512 devices in a mesh: group: 32 (over z_hi, x, core), tp: 16 (over z_lo, y).
Axes of the slice: x: 4, y: 4, z: 16 (z_hi: 4, z_lo: 4; z = z_hi * 4 + z_lo), core: 2. Of those that a mesh axis runs over, the one named last changes fastest.
Arguments:
- queries: bfloat16 [512, 4096], P('group', 'tp'), may hold values from -45 to 45
- new_key: bfloat16 [512, 4, 128], P('group'), may hold values from -12 to 12
- new_value: bfloat16 [512, 4, 128], P('group'), may hold values from -6 to 6
- lengths: int32 [512], P('group'), may hold values from 1 to 16384, as said below
- slot_row: int32 [32, 64], P('group'), may hold values from 0 to 15
- slot_block: int32 [32, 64], P('group'), may hold values from 0 to 32, as said below
- key_cache: bfloat16 [32, 64, 16, 128, 128], P('group', None, 'tp'), may hold values from -12 to 12
- value_cache: bfloat16 [32, 64, 16, 128, 128], P('group', None, 'tp'), may hold values from -6 to 6
Outputs:
- attended: bfloat16 [512, 4096], P('group', 'tp')
The draws below stay inside these ranges and needn't reach their ends.
Inputs may be any that keep to these rules, and one draw needn't show every extreme that they name: `lengths`: the largest length is 16384, reached in every group. A rollout of n cached tokens has its blocks 0 to ceil(n / 512) - 1 each in exactly one slot with owner its group, on any group; every other slot holds block index 32. `slot_block`: empty slots hold 32.
All inputs are finite; a program needn't handle non-finite values.
Results may differ from the reference program's by a relative error of at most 0.0021.
Values may be sent and summed in bfloat16 or wider, within the bound.
A program may use at most 64 MiB of HBM per device.

```python
import jax
import jax.numpy as jnp
from jax import lax

QH = 32
KVH = 4
HD = 128
BLK = 512
SEQ_DEV = 16
HELPERS = 32
SHARES = 16
SUB = 128
PER = 2
SLOTS = 64
MAXBLK = 32
SEQS = 512


def owner_layout(key):
    keys_list = jax.random.split(key, 5)
    row_ids = jnp.arange(SEQ_DEV, dtype=jnp.int32)
    long_row = jax.random.randint(keys_list[0], (), 0, SEQ_DEV)
    spare = SLOTS - MAXBLK - (SEQ_DEV - 1)
    extras = jax.random.randint(keys_list[1], (), spare // 2, spare)
    picks = jax.random.randint(keys_list[2], (spare,), 0, SEQ_DEV - 1)
    picks = picks + (picks >= long_row).astype(jnp.int32)
    active = (jnp.arange(spare, dtype=jnp.int32) < extras).astype(jnp.int32)
    counts = 1 + jnp.sum((picks[:, None] == row_ids[None, :]).astype(jnp.int32) * active[:, None], axis=0)
    counts = jnp.where(row_ids == long_row, MAXBLK, counts)
    last_fill = jax.random.randint(keys_list[3], (SEQ_DEV,), 1, BLK + 1)
    lens = jnp.where(row_ids == long_row, MAXBLK * BLK, (counts - 1) * BLK + last_fill)
    starts = jnp.cumsum(counts) - counts
    total = jnp.sum(counts)
    listed = jnp.arange(SLOTS, dtype=jnp.int32)
    row_of = jnp.sum((listed[:, None] >= starts[None, :]).astype(jnp.int32), axis=1) - 1
    block_of = listed - starts[row_of]
    filled = listed < total
    row_of = jnp.where(filled, row_of, listed % SEQ_DEV)
    block_of = jnp.where(filled, block_of, MAXBLK)
    order = jax.random.permutation(keys_list[4], SLOTS)
    row_table = jnp.zeros((SLOTS,), jnp.int32).at[order].set(row_of)
    block_table = jnp.zeros((SLOTS,), jnp.int32).at[order].set(block_of)
    return (lens, row_table, block_table)


def block_layout(key):
    owner_keys = jax.random.split(jax.random.fold_in(key, 101), HELPERS)
    lens, row_table, block_table = jax.vmap(owner_layout)(owner_keys)
    row_table = row_table.reshape(HELPERS, HELPERS, PER).transpose(1, 0, 2).reshape(HELPERS, SLOTS)
    block_table = block_table.reshape(HELPERS, HELPERS, PER).transpose(1, 0, 2).reshape(HELPERS, SLOTS)
    return (lens.reshape(SEQS), row_table, block_table)


def draw_lengths(key, part):
    return block_layout(key)[0]


def draw_slot_row(key, part):
    return block_layout(key)[1]


def draw_slot_block(key, part):
    return block_layout(key)[2]


def draw_queries(key, part):
    key = jax.random.fold_in(key, 7)
    first = jax.random.fold_in(key, 0)
    values = jnp.clip(jax.random.normal(first, (SEQS, QH * HD), jnp.float32), -6.0, 6.0)
    return values.astype(jnp.bfloat16)


def draw_key_cache(key, part):
    key = jax.random.fold_in(key, 11)
    first = jax.random.fold_in(key, 0)
    shape = (HELPERS, SLOTS, SHARES, SUB, HD)
    values = jnp.clip(3.0 * jax.random.normal(first, shape, jnp.float32), -12.0, 12.0)
    return values.astype(jnp.bfloat16)


def shard_levels(key, dims, shards, least, high):
    def one(position, parts):
        heights = jax.random.uniform(jax.random.fold_in(jax.random.fold_in(key, 6), position), (parts,), jnp.float32, least / len(shards), high / len(shards))
        return jnp.repeat(jnp.exp(heights), dims[position] // parts).reshape((-1,) + (1,) * (len(dims) - position - 1))

    loudness = one(*shards[0])
    for cut in shards[1:]:
        loudness = loudness * one(*cut)
    return loudness


def gaussian(own_key, extent, deviation, most, cuts=(), held_as=jnp.bfloat16):
    array = deviation * jax.random.normal(own_key, extent, jnp.float32)
    if cuts:
        array = array * shard_levels(own_key, extent, cuts, -0.22, 0.18)
    return jnp.clip(array, -most, most).astype(held_as)


def setup_inputs(seed: int = 0) -> dict:
    key_list = jax.random.split(jax.random.key(seed), 9)
    queries = draw_queries(jax.random.fold_in(key_list[8], 71), 0)
    new_key = gaussian(key_list[1], (SEQS, KVH, HD), 3.0, 12.0, ((0, 32),))
    new_value = gaussian(key_list[2], (SEQS, KVH, HD), 1.0, 6.0, ((0, 32),))
    lengths = draw_lengths(jax.random.fold_in(key_list[8], 71), 0)
    slot_row = draw_slot_row(jax.random.fold_in(key_list[8], 71), 0)
    slot_block = draw_slot_block(jax.random.fold_in(key_list[8], 71), 0)
    key_cache = draw_key_cache(jax.random.fold_in(key_list[8], 71), 0)
    value_cache = gaussian(key_list[7], (HELPERS, SLOTS, SHARES, SUB, HD), 1.0, 6.0, ((0, 32), (2, 16)))
    return {"queries": queries, "new_key": new_key, "new_value": new_value, "lengths": lengths, "slot_row": slot_row, "slot_block": slot_block, "key_cache": key_cache, "value_cache": value_cache}


def reference(queries, new_key, new_value, lengths, slot_row, slot_block, key_cache, value_cache):
    helpers = key_cache.shape[0]
    slot_count = key_cache.shape[1]
    share_count = key_cache.shape[2]
    sub_len = key_cache.shape[3]
    per_pair = slot_count // helpers
    pieces = share_count // KVH
    group_heads = QH // KVH
    seq_total = queries.shape[0]
    seq_per = seq_total // helpers
    score_scale = HD ** -0.5
    queries_f = queries.astype(jnp.float32).reshape(seq_total, KVH, group_heads, HD)
    owners = jnp.arange(slot_count, dtype=jnp.int32) // per_pair
    head_of = jnp.arange(share_count, dtype=jnp.int32) % KVH
    piece_of = jnp.arange(share_count, dtype=jnp.int32) // KVH
    offsets = jnp.arange(sub_len, dtype=jnp.int32)

    def one_helper(packed):
        rows_local, blocks, keys_here, values_here = packed
        seq_rows = (owners * seq_per + rows_local).astype(jnp.int32)
        chosen = queries_f[seq_rows][:, head_of]
        scores = jnp.einsum('kcgd,kcpd->kcgp', chosen, keys_here.astype(jnp.float32)) * score_scale
        places = blocks[:, None, None] * BLK + piece_of[None, :, None] * sub_len + offsets[None, None, :]
        valid = (places < lengths[seq_rows][:, None, None])[:, :, None, :]
        masked = jnp.where(valid, scores, -1e30)
        block_max = jnp.max(masked, axis=3)
        probs = jnp.where(valid, jnp.exp(masked - block_max[..., None]), 0.0)
        block_sum = jnp.sum(probs, axis=3)
        rounded = lax.optimization_barrier(probs.astype(jnp.bfloat16)).astype(jnp.float32)
        block_out = jnp.einsum('kcgp,kcpd->kcgd', rounded, values_here.astype(jnp.float32))
        return block_max, block_sum, block_out, seq_rows

    block_max, block_sum, block_out, seq_rows = lax.map(one_helper, (slot_row, slot_block, key_cache, value_cache))
    flat_rows = seq_rows.reshape(-1)
    block_max = block_max.reshape(helpers * slot_count, share_count, group_heads)
    block_sum = block_sum.reshape(helpers * slot_count, share_count, group_heads)
    block_out = block_out.reshape(helpers * slot_count, share_count, group_heads, HD)
    seg_max = jax.ops.segment_max(block_max, flat_rows, num_segments=seq_total)
    cache_top = jnp.max(seg_max.reshape(seq_total, pieces, KVH, group_heads), axis=1)
    new_score = jnp.einsum('skgd,skd->skg', queries_f, new_key.astype(jnp.float32)) * score_scale
    top_all = jnp.maximum(cache_top, new_score)
    weights = jnp.exp(block_max - top_all[flat_rows][:, head_of])
    numer = jax.ops.segment_sum(block_out * weights[..., None], flat_rows, num_segments=seq_total)
    numer = jnp.sum(numer.reshape(seq_total, pieces, KVH, group_heads, HD), axis=1)
    denom = jax.ops.segment_sum(block_sum * weights, flat_rows, num_segments=seq_total)
    denom = jnp.sum(denom.reshape(seq_total, pieces, KVH, group_heads), axis=1)
    fresh = jnp.exp(new_score - top_all)
    numer = numer + fresh[..., None] * new_value.astype(jnp.float32)[:, :, None, :]
    denom = denom + fresh
    return (numer / denom[..., None]).reshape(seq_total, QH * HD).astype(jnp.bfloat16)
```

```python
import functools

import jax
import jax.numpy as jnp
from jax import lax
from jax.experimental import pallas as pl
from jax.experimental.pallas import tpu as pltpu
from jax.sharding import PartitionSpec as P

QH = 32
KVH = 4
HD = 128
BLK = 512
SUB = 128
NZ = 4
NP = 8
NU = 4
NW = 4
ROWS = 16
PER = 2
SCALE = HD ** (-0.5)
LOW = -1e30
MESH = pl.DeviceIdType.MESH
F32 = jnp.float32
BF16 = jnp.bfloat16


def iota(shape, dim):
    return lax.broadcasted_iota(jnp.int32, shape, dim)


def kernel(
    q_ref, nk_ref, nv_ref, len_ref, row_ref, blk_ref, key_ref, value_ref, out_ref,
    kbuf, vbuf, qsend, qb, lsend, lb, tsend, tb, s2, qr, lr, osend, ssend, orecv, srecv, fos, fss, fo, fs,
    local_sem, send_sem, recv_sem, chunk_sem, chunk_len_sem,
):
    g = lax.axis_index("group")
    t = lax.axis_index("tp")
    z0, p0 = g // NP, lax.rem(g, NP)
    u, w = t // NW, lax.rem(t, NW)
    diagonal = u == w

    def place(zz, pp, uu, ww):
        return (zz * NP + pp, uu * NW + ww)

    key_copy = pltpu.make_async_copy(key_ref.at[0, :, 0], kbuf, local_sem.at[0])
    value_copy = pltpu.make_async_copy(value_ref.at[0, :, 0], vbuf, local_sem.at[1])
    key_copy.start()
    value_copy.start()

    barrier = pltpu.get_barrier_semaphore()

    def greet_far(d, carry):
        target = place(d // NW, p0, w, lax.rem(d, NW))

        @pl.when(jnp.logical_or(target[0] != g, target[1] != t))
        def _():
            pl.semaphore_signal(barrier, inc=1, device_id=target, device_id_type=MESH)

        return carry

    lax.fori_loop(0, NZ * NW, greet_far, 0)

    def greet_plane(d, carry):
        target = place(z0, d // NU, lax.rem(d, NU), w)

        @pl.when(jnp.logical_or(target[0] != g, target[1] != t))
        def _():
            pl.semaphore_signal(barrier, inc=1, device_id=target, device_id_type=MESH)

        return carry

    lax.fori_loop(0, NP * NU, greet_plane, 0)

    qsend[0:ROWS, :] = q_ref[:, 0:HD]
    qsend[ROWS : 2 * ROWS, :] = q_ref[:, HD : 2 * HD]
    lane1 = iota((1, HD), 1)
    lens = jnp.zeros((1, HD), jnp.int32)
    for r in range(ROWS):
        lens = jnp.where(lane1 == r, len_ref[r], lens)
    lsend[...] = lens
    for p in range(NP):
        row = jnp.zeros((1, HD), jnp.int32)
        for zz in range(NZ):
            for s in range(PER):
                row = jnp.where(
                    lane1 // 2 == p0 * 8 + zz * 2 + s, row_ref[0, (zz * NP + p) * PER + s], row
                )
        tsend[p] = row

    pl.semaphore_wait(barrier, NZ * NW + NP * NU - 1 - jnp.where(diagonal, 1, 0))

    def send(src, dst, target, which, recv):
        here = jnp.logical_and(target[0] == g, target[1] == t)

        @pl.when(jnp.logical_not(here))
        def _():
            pltpu.make_async_remote_copy(
                src_ref=src,
                dst_ref=dst,
                send_sem=send_sem.at[which],
                recv_sem=recv,
                device_id=target,
                device_id_type=MESH,
            ).start()

        @pl.when(here)
        def _():
            pltpu.make_async_copy(src, dst, recv).start()

    def a1(d, carry):
        zd, bd = d // NU, lax.rem(d, NU)
        send(qsend, qb.at[z0, pl.ds(pl.multiple_of(w * 32, 32), 32)], place(zd, p0, bd, u), 0, recv_sem.at[0])
        return carry

    lax.fori_loop(0, NZ * NU, a1, 0)

    def a1_lens(zd, carry):
        send(lsend, lb.at[z0], place(zd, p0, w, u), 1, recv_sem.at[1])
        return carry

    lax.fori_loop(0, NZ, a1_lens, 0)

    def table(pd, carry):
        send(tsend.at[pd], tb.at[p0], place(z0, pd, u, w), 2, recv_sem.at[2])
        return carry

    lax.fori_loop(0, NP, table, 0)
    pltpu.make_async_copy(tb, tb, recv_sem.at[2]).wait()

    rows = jnp.sum(tb[...], axis=0)
    sub = iota((HD, HD), 0)
    lane = iota((HD, HD), 1)
    head_match = lane // ROWS == 2 * (lax.rem(sub, 16) // 4) + lax.rem(sub, 2)
    lane_row = lax.rem(lane, ROWS)
    picks = []
    for zz in range(NZ):
        at = (sub // 16) * 16 + zz * 4 + lax.rem(sub, 4)
        wanted = jnp.sum(jnp.where(lane == at, rows, 0), axis=1, keepdims=True)
        picks.append(jnp.where(jnp.logical_and(head_match, lane_row == wanted), 1.0, 0.0).astype(BF16))

    nk = nk_ref[...].astype(F32)
    nv = nv_ref[...].astype(F32)
    fresh_key = jnp.zeros((ROWS, HD), F32)
    fresh_value = jnp.zeros((ROWS, HD), F32)
    for k in range(KVH):
        fresh_key = jnp.where(u == k, nk[:, k, :], fresh_key)
        fresh_value = jnp.where(u == k, nv[:, k, :], fresh_value)
    fresh_key = jnp.concatenate([fresh_key, fresh_key], axis=0)
    fresh_value = jnp.concatenate([fresh_value, fresh_value], axis=0)
    new_score = jnp.sum(qsend[...].astype(F32) * fresh_key, axis=1, keepdims=True) * SCALE

    pltpu.make_async_copy(qb, qb, recv_sem.at[0]).wait()
    pltpu.make_async_copy(lb, lb, recv_sem.at[1]).wait()
    for zz in range(NZ):
        chosen = jnp.dot(picks[zz], qb[zz], preferred_element_type=F32).astype(BF16)
        s2[:, zz] = chosen.reshape(NP, 16, HD)

    def a2(d, carry):
        pd = lax.rem(p0 + d, NP)
        send(s2.at[pd], qr.at[p0], place(z0, pd, u, w), 3, chunk_sem.at[p0])
        send(lb, lr.at[p0], place(z0, pd, u, w), 4, chunk_len_sem.at[p0])
        return carry

    lax.fori_loop(0, NP, a2, 0)
    key_copy.wait()
    value_copy.wait()

    row16 = iota((16, 2 * SUB), 0)
    lane2 = iota((16, 2 * SUB), 1)
    second = lax.rem(row16, 4) // 2
    token = jnp.where(second == lane2 // SUB, lax.rem(lane2, SUB), 1 << 20)
    second_col = lax.rem(iota((16, 1), 0), 4) // 2
    spot = iota((16, HD), 1) - p0 * 16 - lax.rem(iota((16, HD), 0), 4)

    def chunk(d, carry):
        p = lax.rem(p0 + d, NP)
        pltpu.make_async_copy(qr.at[p], qr.at[p], chunk_sem.at[p]).wait()
        pltpu.make_async_copy(lr.at[p], lr.at[p], chunk_len_sem.at[p]).wait()
        outs = []
        place_max = jnp.zeros((16, HD), F32)
        place_sum = jnp.zeros((16, HD), F32)
        for zz in range(NZ):
            slot = (zz * NP + p) * PER
            keys = kbuf[pl.ds(slot, PER)].reshape(PER * SUB, HD)
            values = vbuf[pl.ds(slot, PER)].reshape(PER * SUB, HD)
            score = (
                lax.dot_general(
                    qr[p, zz], keys, (((1,), (1,)), ((), ())), preferred_element_type=F32
                )
                * SCALE
            )
            live = []
            for s in range(PER):
                length = jnp.sum(
                    jnp.where(lane1 == row_ref[0, slot + s], lr[p, zz], 0), axis=1, keepdims=True
                )
                live.append(length - (blk_ref[0, slot + s] * BLK + u * SUB))
            valid = token < jnp.where(second_col == 0, live[0], live[1])
            masked = jnp.where(valid, score, LOW)
            top = jnp.max(masked, axis=1, keepdims=True)
            prob = jnp.where(valid, jnp.exp(masked - top), 0.0)
            total = jnp.sum(prob, axis=1, keepdims=True)
            outs.append(jnp.dot(prob.astype(BF16), values, preferred_element_type=F32))
            place_max = jnp.where(spot == zz * 4, top, place_max)
            place_sum = jnp.where(spot == zz * 4, total, place_sum)
        for j in range(NU):
            part = slice(4 * j, 4 * j + 4)
            osend[p, j] = jnp.concatenate([o[part] for o in outs], axis=0)
            ssend[p, j] = jnp.concatenate(
                [
                    jnp.sum(place_max[part], axis=0, keepdims=True),
                    jnp.sum(place_sum[part], axis=0, keepdims=True),
                ],
                axis=0,
            )

        def b1(j, inner):
            target = place(z0, p, j, w)
            send(osend.at[p, j], orecv.at[u * NP + p0], target, 5, recv_sem.at[3])
            send(ssend.at[p, j], srecv.at[u * NP + p0], target, 6, recv_sem.at[4])
            return inner

        lax.fori_loop(0, NU, b1, 0)
        return carry

    lax.fori_loop(0, NP, chunk, 0)

    match = jnp.logical_and(
        sub // 32 == lax.rem(lane, 16) // 4,
        jnp.logical_and(lax.rem(sub // 16, 2) == lax.rem(lane, 2), lax.rem(sub, 16) == rows),
    )
    pltpu.make_async_copy(srecv, srecv, recv_sem.at[4]).wait()
    tops, totals = [], []
    for b in range(NU):
        stats = jnp.sum(srecv[b * NP : (b + 1) * NP], axis=0)
        tops.append(jnp.where(match, stats[0:1], LOW))
        totals.append(stats[1:2])
    plane_top = jnp.max(
        jnp.maximum(jnp.maximum(tops[0], tops[1]), jnp.maximum(tops[2], tops[3])), axis=1, keepdims=True
    )
    weights = [jnp.where(match, jnp.exp(m - plane_top), 0.0) for m in tops]
    plane_sum = jnp.sum(sum(x * y for x, y in zip(weights, totals)), axis=1, keepdims=True)
    pltpu.make_async_copy(orecv, orecv, recv_sem.at[3]).wait()
    plane_out = jnp.zeros((HD, HD), F32)
    for b in range(NU):
        plane_out += jnp.dot(
            weights[b],
            orecv[b * NP : (b + 1) * NP].reshape(NP * 16, HD),
            precision=lax.Precision.HIGHEST,
            preferred_element_type=F32,
        )
    fos[...] = plane_out.reshape(NZ, 32, HD)
    packed = jnp.where(lane == lax.rem(sub, 32), plane_top, 0.0)
    packed = jnp.where(lane == 32 + lax.rem(sub, 32), plane_sum, packed)
    fss[...] = jnp.sum(packed.reshape(NZ, 32, HD), axis=1, keepdims=True)

    def b2(zd, carry):
        target = place(zd, p0, w, u)
        send(fos.at[zd], fo.at[z0], target, 7, recv_sem.at[5])
        send(fss.at[zd], fs.at[z0], target, 8, recv_sem.at[6])
        return carry

    lax.fori_loop(0, NZ, b2, 0)

    sub32 = iota((32, HD), 0)
    lane32 = iota((32, HD), 1)
    pltpu.make_async_copy(fs, fs, recv_sem.at[6]).wait()
    part_tops, part_sums = [], []
    for zz in range(NZ):
        part_tops.append(jnp.sum(jnp.where(lane32 == sub32, fs[zz], 0.0), axis=1, keepdims=True))
        part_sums.append(jnp.sum(jnp.where(lane32 == 32 + sub32, fs[zz], 0.0), axis=1, keepdims=True))
    last_top = new_score
    for m in part_tops:
        last_top = jnp.maximum(last_top, m)
    fresh = jnp.exp(new_score - last_top)
    denom = fresh
    numer = fresh * fresh_value
    factors = [jnp.exp(m - last_top) for m in part_tops]
    for zz in range(NZ):
        denom += factors[zz] * part_sums[zz]
    pltpu.make_async_copy(fo, fo, recv_sem.at[5]).wait()
    for zz in range(NZ):
        numer += factors[zz] * fo[zz]
    result = (numer / denom).astype(BF16)
    out_ref[:, 0:HD] = result[0:ROWS]
    out_ref[:, HD : 2 * HD] = result[ROWS : 2 * ROWS]

    def sent(ref, which):
        pltpu.make_async_copy(ref, ref, send_sem.at[which]).wait()

    def sent_unless_diagonal(ref, which):
        @pl.when(jnp.logical_not(diagonal))
        def _():
            sent(ref, which)

    blocks = qb.at[pl.ds(0, 3)]
    sent(blocks, 0)
    sent(qb.at[3, pl.ds(0, 96)], 0)
    sent_unless_diagonal(qsend, 0)
    sent(lb.at[pl.ds(0, 3)], 1)
    sent_unless_diagonal(lsend, 1)
    sent(tb.at[pl.ds(0, NP - 1)], 2)
    sent(qr.at[pl.ds(0, NP - 1)], 3)
    sent(lr.at[pl.ds(0, NP - 1)], 4)
    sent(orecv.at[pl.ds(0, NP * NU - 1)], 5)
    sent(srecv.at[pl.ds(0, NP * NU - 1)], 6)
    sent(fo.at[pl.ds(0, NZ - 1)], 7)
    sent_unless_diagonal(fo.at[0], 7)
    sent(fs.at[pl.ds(0, NZ - 1)], 8)
    sent_unless_diagonal(fs.at[0], 8)


def on_device(queries, new_key, new_value, lengths, slot_row, slot_block, key_cache, value_cache):
    vmem = pl.BlockSpec(memory_space=pltpu.VMEM)
    smem = pl.BlockSpec(memory_space=pltpu.SMEM)
    anywhere = pl.BlockSpec(memory_space=pl.ANY)
    slots = NZ * NP * PER
    return pl.pallas_call(
        kernel,
        out_shape=jax.ShapeDtypeStruct((ROWS, 2 * HD), BF16),
        in_specs=[vmem, vmem, vmem, smem, smem, smem, anywhere, anywhere],
        out_specs=vmem,
        scratch_shapes=[
            pltpu.VMEM((slots, SUB, HD), BF16),
            pltpu.VMEM((slots, SUB, HD), BF16),
            pltpu.VMEM((2 * ROWS, HD), BF16),
            pltpu.VMEM((NZ, HD, HD), BF16),
            pltpu.VMEM((1, HD), jnp.int32),
            pltpu.VMEM((NZ, 1, HD), jnp.int32),
            pltpu.VMEM((NP, 1, HD), jnp.int32),
            pltpu.VMEM((NP, 1, HD), jnp.int32),
            pltpu.VMEM((NP, NZ, 16, HD), BF16),
            pltpu.VMEM((NP, NZ, 16, HD), BF16),
            pltpu.VMEM((NP, NZ, 1, HD), jnp.int32),
            pltpu.VMEM((NP, NU, 16, HD), F32),
            pltpu.VMEM((NP, NU, 2, HD), F32),
            pltpu.VMEM((NU * NP, 16, HD), F32),
            pltpu.VMEM((NU * NP, 2, HD), F32),
            pltpu.VMEM((NZ, 32, HD), F32),
            pltpu.VMEM((NZ, 1, HD), F32),
            pltpu.VMEM((NZ, 32, HD), F32),
            pltpu.VMEM((NZ, 1, HD), F32),
            pltpu.SemaphoreType.DMA((2,)),
            pltpu.SemaphoreType.DMA((9,)),
            pltpu.SemaphoreType.DMA((7,)),
            pltpu.SemaphoreType.DMA((NP,)),
            pltpu.SemaphoreType.DMA((NP,)),
        ],
        compiler_params=pltpu.CompilerParams(
            collective_id=0, has_side_effects=True, vmem_limit_bytes=32 * 1024 * 1024
        ),
        cost_estimate=pl.CostEstimate(flops=2 * 2 * 2 * 8 * slots * SUB * HD, bytes_accessed=2 * slots * SUB * HD * 2, transcendentals=slots * 16 * SUB),
    )(queries, new_key, new_value, lengths, slot_row, slot_block, key_cache, value_cache)


def solution(mesh):
    in_specs = (
        P("group", "tp"),
        P("group", None, None),
        P("group", None, None),
        P("group"),
        P("group", None),
        P("group", None),
        P("group", None, "tp", None, None),
        P("group", None, "tp", None, None),
    )
    return jax.shard_map(
        on_device, mesh=mesh, in_specs=in_specs, out_specs=P("group", "tp"), check_vma=False
    )
```

```python
import functools

import jax
import jax.numpy as jnp
from jax import lax
from jax.experimental import pallas as pl
from jax.experimental.pallas import tpu as pltpu
from jax.sharding import PartitionSpec as P

QH = 32
KVH = 4
HD = 128
BLK = 512
SUB = 128
NZ = 4
NP = 8
NU = 4
NW = 4
ROWS = 16
PER = 2
SCALE = HD ** (-0.5)
LOW = -1e30
MESH = pl.DeviceIdType.MESH
F32 = jnp.float32
BF16 = jnp.bfloat16


def iota(shape, dim):
    return lax.broadcasted_iota(jnp.int32, shape, dim)


def kernel(
    q_hbm, nk_hbm, nv_hbm, len_hbm, row_hbm, blk_hbm, key_hbm, value_hbm, out_ref,
    q_ref, nk_ref, nv_ref, len_ref, row_ref, blk_ref, kbuf, vbuf,
    qsend, qb, lsend, lb, tsend, tb, s2, qr, osend, ssend, orecv, srecv, fos, fss, fo, fs,
    local_sem, send_sem, recv_sem, chunk_sem,
):
    g = lax.axis_index("group")
    t = lax.axis_index("tp")
    z0, p0 = g // NP, lax.rem(g, NP)
    u, w = t // NW, lax.rem(t, NW)
    diagonal = u == w

    def place(zz, pp, uu, ww):
        return (zz * NP + pp, uu * NW + ww)

    barrier = pltpu.get_barrier_semaphore()

    def greet(target):
        pl.semaphore_signal(barrier, inc=1, device_id=target, device_id_type=MESH)

    def greet_far(d, carry):
        target = place(lax.rem(z0 + 2 + d // NW, NZ), p0, w, lax.rem(d, NW))

        @pl.when(jnp.logical_or(target[0] != g, target[1] != t))
        def _():
            greet(target)

        return carry

    lax.fori_loop(0, NZ * NW, greet_far, 0)
    small = [
        pltpu.make_async_copy(src, dst, local_sem.at[i])
        for i, (src, dst) in enumerate(
            ((q_hbm, q_ref), (len_hbm, len_ref), (row_hbm, row_ref), (blk_hbm, blk_ref), (nk_hbm, nk_ref), (nv_hbm, nv_ref))
        )
    ]
    key_copy = pltpu.make_async_copy(key_hbm.at[0, :, 0], kbuf, local_sem.at[6])
    value_copy = pltpu.make_async_copy(value_hbm.at[0, :, 0], vbuf, local_sem.at[7])
    for copy in small[:4]:
        copy.start()

    def greet_plane(d, carry):
        greet(place(z0, lax.rem(p0 + d, NP), u, w))
        return carry

    lax.fori_loop(1, NP, greet_plane, 0)
    for d in range(1, NU):
        greet(place(z0, p0, lax.rem(u + d, NU), w))
    for copy in (*small[4:], key_copy, value_copy):
        copy.start()
    for copy in small[:4]:
        copy.wait()

    qsend[0:ROWS, :] = q_ref[:, 0:HD]
    qsend[ROWS : 2 * ROWS, :] = q_ref[:, HD : 2 * HD]
    lane1 = iota((1, HD), 1)
    lens = jnp.zeros((1, HD), jnp.int32)
    for r in range(ROWS):
        lens = jnp.where(lane1 == r, len_ref[r], lens)
    lsend[...] = lens
    for p in range(NP):
        row = jnp.zeros((1, HD), jnp.int32)
        for zz in range(NZ):
            for s in range(PER):
                row = jnp.where(
                    lane1 // 2 == p0 * 8 + zz * 2 + s, row_ref[0, (zz * NP + p) * PER + s], row
                )
        tsend[p] = row

    pl.semaphore_wait(barrier, NZ * NW + NP - 1 + NU - 1 - jnp.where(diagonal, 1, 0))

    def send(src, dst, target, which, recv):
        here = jnp.logical_and(target[0] == g, target[1] == t)

        @pl.when(jnp.logical_not(here))
        def _():
            pltpu.make_async_remote_copy(
                src_ref=src,
                dst_ref=dst,
                send_sem=send_sem.at[which],
                recv_sem=recv,
                device_id=target,
                device_id_type=MESH,
            ).start()

        @pl.when(here)
        def _():
            pltpu.make_async_copy(src, dst, recv).start()

    def a1(d, carry):
        zd, bd = lax.rem(z0 + 2 + d // NU, NZ), lax.rem(d, NU)
        send(qsend, qb.at[z0, pl.ds(pl.multiple_of(w * 32, 32), 32)], place(zd, p0, bd, u), 0, recv_sem.at[0])
        return carry

    lax.fori_loop(0, NZ * NU, a1, 0)

    def a1_lens(zd, carry):
        send(lsend, lb.at[z0], place(zd, p0, w, u), 1, recv_sem.at[1])
        return carry

    lax.fori_loop(0, NZ, a1_lens, 0)

    def table(pd, carry):
        send(tsend.at[pd], tb.at[p0], place(z0, pd, u, w), 2, recv_sem.at[2])
        return carry

    lax.fori_loop(0, NP, table, 0)
    pltpu.make_async_copy(tb, tb, recv_sem.at[2]).wait()

    rows = jnp.sum(tb[...], axis=0)
    sub = iota((HD, HD), 0)
    lane = iota((HD, HD), 1)
    head_match = lane // ROWS == 2 * (lax.rem(sub, 16) // 4) + lax.rem(sub, 2)
    lane_row = lax.rem(lane, ROWS)
    picks = []
    for zz in range(NZ):
        at = (sub // 16) * 16 + zz * 4 + lax.rem(sub, 4)
        wanted = jnp.sum(jnp.where(lane == at, rows, 0), axis=1, keepdims=True)
        picks.append(jnp.where(jnp.logical_and(head_match, lane_row == wanted), 1.0, 0.0).astype(BF16))

    small[4].wait()
    small[5].wait()
    nk = nk_ref[...].astype(F32)
    nv = nv_ref[...].astype(F32)
    fresh_key = jnp.zeros((ROWS, HD), F32)
    fresh_value = jnp.zeros((ROWS, HD), F32)
    for k in range(KVH):
        fresh_key = jnp.where(u == k, nk[:, k, :], fresh_key)
        fresh_value = jnp.where(u == k, nv[:, k, :], fresh_value)
    fresh_key = jnp.concatenate([fresh_key, fresh_key], axis=0)
    fresh_value = jnp.concatenate([fresh_value, fresh_value], axis=0)
    new_score = jnp.sum(qsend[...].astype(F32) * fresh_key, axis=1, keepdims=True) * SCALE

    pltpu.make_async_copy(qb, qb, recv_sem.at[0]).wait()
    pltpu.make_async_copy(lb, lb, recv_sem.at[1]).wait()
    for zz in range(NZ):
        chosen = jnp.dot(picks[zz], qb[zz], preferred_element_type=F32).astype(BF16)
        s2[:, zz * 16 : zz * 16 + 16] = chosen.reshape(NP, 16, HD)
    lens = jnp.concatenate([lb[zz] for zz in range(NZ)] + [jnp.zeros((16 - NZ, HD), jnp.int32)], axis=0)
    low = pltpu.roll(lax.rem(lens, 128), 16, 1)
    coded = jnp.where(iota((16, HD), 1) < ROWS, lens // 128, low).astype(F32).astype(BF16)
    s2[:, NZ * 16 : NZ * 16 + 16] = jnp.broadcast_to(coded[None], (NP, 16, HD))

    def a2(d, carry):
        pd = lax.rem(p0 + d, NP)
        send(s2.at[pd], qr.at[p0], place(z0, pd, u, w), 3, chunk_sem.at[p0])
        return carry

    lax.fori_loop(0, NP, a2, 0)
    key_copy.wait()
    value_copy.wait()

    row32 = iota((32, 2 * SUB), 0)
    lane2 = iota((32, 2 * SUB), 1)
    second = lax.rem(row32, 4) // 2
    token = jnp.where(second == lane2 // SUB, lax.rem(lane2, SUB), 1 << 20)
    second_col = lax.rem(iota((16, 1), 0), 4) // 2
    spot = iota((16, HD), 1) - p0 * 16 - lax.rem(iota((16, HD), 0), 4)
    no_query = jnp.zeros((16, HD), BF16)

    def chunk(d, carry):
        p = lax.rem(p0 + d, NP)
        pltpu.make_async_copy(qr.at[p], qr.at[p], chunk_sem.at[p]).wait()
        coded = qr[p, NZ * 16 : NZ * 16 + 16].astype(F32)
        outs, tops, totals = [], [], []

        def limit(zz):
            slot = (zz * NP + p) * PER
            live = []
            for s in range(PER):
                row = row_ref[0, slot + s]
                parts = jnp.where(lane1 == row, coded[zz : zz + 1] * 128.0, 0.0)
                parts = jnp.where(lane1 == row + ROWS, coded[zz : zz + 1], parts)
                length = jnp.sum(parts, axis=1, keepdims=True).astype(jnp.int32)
                live.append(length - (blk_ref[0, slot + s] * BLK + u * SUB))
            return jnp.where(second_col == 0, live[0], live[1])

        def pair(ref, za, zb):
            halves = [ref[pl.ds((zz * NP + p) * PER, PER)].reshape(PER * SUB, HD) for zz in (za, zb)]
            return jnp.concatenate(halves, axis=1)

        for za, zb in ((0, 1), (2, 3)):
            query = jnp.concatenate(
                [
                    jnp.concatenate([qr[p, za * 16 : za * 16 + 16], no_query], axis=1),
                    jnp.concatenate([no_query, qr[p, zb * 16 : zb * 16 + 16]], axis=1),
                ],
                axis=0,
            )
            score = (
                lax.dot_general(
                    query, pair(kbuf, za, zb), (((1,), (1,)), ((), ())), preferred_element_type=F32
                )
                * SCALE
            )
            valid = token < jnp.concatenate([limit(za), limit(zb)], axis=0)
            masked = jnp.where(valid, score, LOW)
            top = jnp.max(masked, axis=1, keepdims=True)
            prob = jnp.where(valid, jnp.exp(masked - top), 0.0)
            total = jnp.sum(prob, axis=1, keepdims=True)
            both = jnp.dot(prob.astype(BF16), pair(vbuf, za, zb), preferred_element_type=F32)
            outs += [both[:16, :HD], both[16:, HD:]]
            tops += [top[:16], top[16:]]
            totals += [total[:16], total[16:]]
        place_max = jnp.zeros((16, HD), F32)
        place_sum = jnp.zeros((16, HD), F32)
        for zz in range(NZ):
            place_max = jnp.where(spot == zz * 4, tops[zz], place_max)
            place_sum = jnp.where(spot == zz * 4, totals[zz], place_sum)
        for j in range(NU):
            part = slice(4 * j, 4 * j + 4)
            osend[p, j] = jnp.concatenate([o[part] for o in outs], axis=0)
            ssend[p, j] = jnp.concatenate(
                [
                    jnp.sum(place_max[part], axis=0, keepdims=True),
                    jnp.sum(place_sum[part], axis=0, keepdims=True),
                ],
                axis=0,
            )

        def b1(j, inner):
            target = place(z0, p, j, w)
            send(osend.at[p, j], orecv.at[u * NP + p0], target, 5, recv_sem.at[3])
            send(ssend.at[p, j], srecv.at[u * NP + p0], target, 6, recv_sem.at[4])
            return inner

        lax.fori_loop(0, NU, b1, 0)
        return carry

    lax.fori_loop(0, NP, chunk, 0)

    match = jnp.logical_and(
        sub // 32 == lax.rem(lane, 16) // 4,
        jnp.logical_and(lax.rem(sub // 16, 2) == lax.rem(lane, 2), lax.rem(sub, 16) == rows),
    )
    pltpu.make_async_copy(srecv, srecv, recv_sem.at[4]).wait()
    tops, totals = [], []
    for b in range(NU):
        stats = jnp.sum(srecv[b * NP : (b + 1) * NP], axis=0)
        tops.append(jnp.where(match, stats[0:1], LOW))
        totals.append(stats[1:2])
    plane_top = jnp.max(
        jnp.maximum(jnp.maximum(tops[0], tops[1]), jnp.maximum(tops[2], tops[3])), axis=1, keepdims=True
    )
    weights = [jnp.where(match, jnp.exp(m - plane_top), 0.0) for m in tops]
    plane_sum = jnp.sum(sum(x * y for x, y in zip(weights, totals)), axis=1, keepdims=True)
    pltpu.make_async_copy(orecv, orecv, recv_sem.at[3]).wait()
    plane_out = jnp.zeros((HD, HD), F32)
    for b in range(NU):
        plane_out += jnp.dot(
            weights[b],
            orecv[b * NP : (b + 1) * NP].reshape(NP * 16, HD),
            precision=lax.Precision.HIGHEST,
            preferred_element_type=F32,
        )
    fos[...] = plane_out.reshape(NZ, 32, HD)
    packed = jnp.where(lane == lax.rem(sub, 32), plane_top, 0.0)
    packed = jnp.where(lane == 32 + lax.rem(sub, 32), plane_sum, packed)
    fss[...] = jnp.sum(packed.reshape(NZ, 32, HD), axis=1, keepdims=True)

    def b2(d, carry):
        zd = lax.rem(z0 + 2 + d, NZ)
        target = place(zd, p0, w, u)
        send(fos.at[zd], fo.at[z0], target, 7, recv_sem.at[5])
        send(fss.at[zd], fs.at[z0], target, 8, recv_sem.at[6])
        return carry

    lax.fori_loop(0, NZ, b2, 0)

    sub32 = iota((32, HD), 0)
    lane32 = iota((32, HD), 1)
    pltpu.make_async_copy(fs, fs, recv_sem.at[6]).wait()
    part_tops, part_sums = [], []
    for zz in range(NZ):
        part_tops.append(jnp.sum(jnp.where(lane32 == sub32, fs[zz], 0.0), axis=1, keepdims=True))
        part_sums.append(jnp.sum(jnp.where(lane32 == 32 + sub32, fs[zz], 0.0), axis=1, keepdims=True))
    last_top = new_score
    for m in part_tops:
        last_top = jnp.maximum(last_top, m)
    fresh = jnp.exp(new_score - last_top)
    denom = fresh
    numer = fresh * fresh_value
    factors = [jnp.exp(m - last_top) for m in part_tops]
    for zz in range(NZ):
        denom += factors[zz] * part_sums[zz]
    pltpu.make_async_copy(fo, fo, recv_sem.at[5]).wait()
    for zz in range(NZ):
        numer += factors[zz] * fo[zz]
    result = (numer / denom).astype(BF16)
    out_ref[:, 0:HD] = result[0:ROWS]
    out_ref[:, HD : 2 * HD] = result[ROWS : 2 * ROWS]

    def sent(ref, which):
        pltpu.make_async_copy(ref, ref, send_sem.at[which]).wait()

    def sent_unless_diagonal(ref, which):
        @pl.when(jnp.logical_not(diagonal))
        def _():
            sent(ref, which)

    blocks = qb.at[pl.ds(0, 3)]
    sent(blocks, 0)
    sent(qb.at[3, pl.ds(0, 96)], 0)
    sent_unless_diagonal(qsend, 0)
    sent(lb.at[pl.ds(0, 3)], 1)
    sent_unless_diagonal(lsend, 1)
    sent(tb.at[pl.ds(0, NP - 1)], 2)
    sent(qr.at[pl.ds(0, NP - 1)], 3)
    sent(orecv.at[pl.ds(0, NP * NU - 1)], 5)
    sent(srecv.at[pl.ds(0, NP * NU - 1)], 6)
    sent(fo.at[pl.ds(0, NZ - 1)], 7)
    sent_unless_diagonal(fo.at[0], 7)
    sent(fs.at[pl.ds(0, NZ - 1)], 8)
    sent_unless_diagonal(fs.at[0], 8)


def on_device(queries, new_key, new_value, lengths, slot_row, slot_block, key_cache, value_cache):
    hbm = pl.BlockSpec(memory_space=pltpu.HBM)
    slots = NZ * NP * PER
    return pl.pallas_call(
        kernel,
        out_shape=jax.ShapeDtypeStruct((ROWS, 2 * HD), BF16),
        in_specs=[hbm] * 8,
        out_specs=pl.BlockSpec(memory_space=pltpu.VMEM),
        scratch_shapes=[
            pltpu.VMEM((ROWS, 2 * HD), BF16),
            pltpu.VMEM((ROWS, KVH, HD), BF16),
            pltpu.VMEM((ROWS, KVH, HD), BF16),
            pltpu.SMEM((ROWS,), jnp.int32),
            pltpu.SMEM((1, slots), jnp.int32),
            pltpu.SMEM((1, slots), jnp.int32),
            pltpu.VMEM((slots, SUB, HD), BF16),
            pltpu.VMEM((slots, SUB, HD), BF16),
            pltpu.VMEM((2 * ROWS, HD), BF16),
            pltpu.VMEM((NZ, HD, HD), BF16),
            pltpu.VMEM((1, HD), jnp.int32),
            pltpu.VMEM((NZ, 1, HD), jnp.int32),
            pltpu.VMEM((NP, 1, HD), jnp.int32),
            pltpu.VMEM((NP, 1, HD), jnp.int32),
            pltpu.VMEM((NP, NZ * 16 + 16, HD), BF16),
            pltpu.VMEM((NP, NZ * 16 + 16, HD), BF16),
            pltpu.VMEM((NP, NU, 16, HD), F32),
            pltpu.VMEM((NP, NU, 2, HD), F32),
            pltpu.VMEM((NU * NP, 16, HD), F32),
            pltpu.VMEM((NU * NP, 2, HD), F32),
            pltpu.VMEM((NZ, 32, HD), F32),
            pltpu.VMEM((NZ, 1, HD), F32),
            pltpu.VMEM((NZ, 32, HD), F32),
            pltpu.VMEM((NZ, 1, HD), F32),
            pltpu.SemaphoreType.DMA((8,)),
            pltpu.SemaphoreType.DMA((9,)),
            pltpu.SemaphoreType.DMA((7,)),
            pltpu.SemaphoreType.DMA((NP,)),
        ],
        compiler_params=pltpu.CompilerParams(
            collective_id=0, has_side_effects=True, vmem_limit_bytes=60 * 1024 * 1024
        ),
        cost_estimate=pl.CostEstimate(flops=2 * 2 * 2 * 8 * slots * SUB * HD, bytes_accessed=2 * slots * SUB * HD * 2, transcendentals=slots * 16 * SUB),
    )(queries, new_key, new_value, lengths, slot_row, slot_block, key_cache, value_cache)


def solution(mesh):
    in_specs = (
        P("group", "tp"),
        P("group", None, None),
        P("group", None, None),
        P("group"),
        P("group", None),
        P("group", None),
        P("group", None, "tp", None, None),
        P("group", None, "tp", None, None),
    )
    return jax.shard_map(
        on_device, mesh=mesh, in_specs=in_specs, out_specs=P("group", "tp"), check_vma=False
    )
```

```python
import functools

import jax
import jax.numpy as jnp
from jax import lax
from jax.experimental import pallas as pl
from jax.experimental.pallas import tpu as pltpu
from jax.sharding import PartitionSpec as P

QH = 32
KVH = 4
HD = 128
BLK = 512
SUB = 128
NZ = 4
NP = 8
NU = 4
NW = 4
ROWS = 16
PER = 2
FIRST = (0,)
REST = (1, 2, 3)
SCALE = HD ** (-0.5)
LOW = -1e30
MESH = pl.DeviceIdType.MESH
F32 = jnp.float32
BF16 = jnp.bfloat16


def iota(shape, dim):
    return lax.broadcasted_iota(jnp.int32, shape, dim)


def kernel(
    q_hbm, nk_hbm, nv_hbm, len_hbm, row_hbm, blk_hbm, key_hbm, value_hbm, out_ref,
    q_ref, nk_ref, nv_ref, len_ref, row_ref, blk_ref, kbuf, vbuf,
    qsend, qb, tsend, tb, qs, ls, qr, lr, first_o, rest_o, first_r, rest_r, fos, fss, fo, fs,
    local_sem, send_sem, recv_sem, chunk_sem, chunk_len_sem,
):
    g = lax.axis_index("group")
    t = lax.axis_index("tp")
    z0, p0 = g // NP, lax.rem(g, NP)
    u, w = t // NW, lax.rem(t, NW)
    diagonal = u == w

    def place(zz, pp, uu, ww):
        return (zz * NP + pp, uu * NW + ww)

    barrier = pltpu.get_barrier_semaphore()

    def greet(target):
        pl.semaphore_signal(barrier, inc=1, device_id=target, device_id_type=MESH)

    for step in (2, 1, 3):
        greet(place(lax.rem(z0 + step, NZ), p0, w, u))

    @pl.when(jnp.logical_not(diagonal))
    def _():
        greet(place(z0, p0, w, u))

    small = [
        pltpu.make_async_copy(src, dst, local_sem.at[i])
        for i, (src, dst) in enumerate(
            ((q_hbm, q_ref), (len_hbm, len_ref), (row_hbm, row_ref), (blk_hbm, blk_ref), (nk_hbm, nk_ref), (nv_hbm, nv_ref))
        )
    ]
    key_copy = pltpu.make_async_copy(key_hbm.at[0, :, 0], kbuf, local_sem.at[6])
    value_copy = pltpu.make_async_copy(value_hbm.at[0, :, 0], vbuf, local_sem.at[7])
    for copy in small[:4]:
        copy.start()

    def greet_plane(d, carry):
        greet(place(z0, lax.rem(p0 + d, NP), u, w))
        return carry

    lax.fori_loop(1, NP, greet_plane, 0)
    for d in range(1, NU):
        greet(place(z0, p0, lax.rem(u + d, NU), w))
    for copy in (*small[4:], key_copy, value_copy):
        copy.start()
    for copy in small[:4]:
        copy.wait()

    qsend[0:ROWS, :] = q_ref[:, 0:HD]
    qsend[ROWS : 2 * ROWS, :] = q_ref[:, HD : 2 * HD]
    lane1 = iota((1, HD), 1)
    lens = jnp.zeros((1, HD), jnp.int32)
    for r in range(ROWS):
        lens = jnp.where(lane1 == r, len_ref[r] // 128, lens)
        lens = jnp.where(lane1 == ROWS + r, lax.rem(len_ref[r], 128), lens)
    qsend[2 * ROWS :, :] = jnp.broadcast_to(lens, (ROWS, HD)).astype(F32).astype(BF16)
    first_spot = jnp.where(lax.rem(lane1, 8) < 4, lax.rem(lane1, 64) // 2, -1)
    for p in range(NP):
        first_row = jnp.zeros((1, HD), jnp.int32)
        rest_row = jnp.zeros((1, HD), jnp.int32)
        for s in range(PER):
            first_row = jnp.where(first_spot == p0 * 4 + s, row_ref[0, p * PER + s], first_row)
            for i, zz in enumerate(REST):
                rest_row = jnp.where(
                    lane1 // 2 == p0 * 8 + i * 2 + s, row_ref[0, (zz * NP + p) * PER + s], rest_row
                )
        tsend[p] = jnp.concatenate([first_row, rest_row], axis=0)

    pl.semaphore_wait(barrier, NZ + NP - 1 + NU - 1 - jnp.where(diagonal, 1, 0))

    def send(src, dst, target, which, recv):
        here = jnp.logical_and(target[0] == g, target[1] == t)

        @pl.when(jnp.logical_not(here))
        def _():
            pltpu.make_async_remote_copy(
                src_ref=src,
                dst_ref=dst,
                send_sem=send_sem.at[which],
                recv_sem=recv,
                device_id=target,
                device_id_type=MESH,
            ).start()

        @pl.when(here)
        def _():
            pltpu.make_async_copy(src, dst, recv).start()

    for step in (2, 1, 3, 0):
        send(qsend, qb.at[z0], place(lax.rem(z0 + step, NZ), p0, w, u), 0, recv_sem.at[0])

    def table(pd, carry):
        send(tsend.at[pd], tb.at[p0], place(z0, pd, u, w), 1, recv_sem.at[1])
        return carry

    lax.fori_loop(0, NP, table, 0)
    pltpu.make_async_copy(tb, tb, recv_sem.at[1]).wait()

    rows = jnp.sum(tb[...], axis=0)
    first_rows, rest_rows = rows[0:1], rows[1:2]
    sub = iota((HD, HD), 0)
    lane = iota((HD, HD), 1)
    at = (sub // 16) * 8 + lax.rem(sub, 16)
    first_wanted = jnp.sum(jnp.where(lane == at, first_rows, 0), axis=1, keepdims=True)
    rest_wanted = jnp.sum(jnp.where(lane == sub - 4, rest_rows, 0), axis=1, keepdims=True)
    wanted = jnp.where(lax.rem(iota((HD, 1), 0), 16) < 4, first_wanted, rest_wanted)
    sub192 = iota((HD, NZ * 48), 0)
    at = (lax.rem(sub192, 16) // 4) * 48 + lax.rem(sub192, 2) * ROWS + wanted
    picks = jnp.where(iota((HD, NZ * 48), 1) == at, 1.0, 0.0).astype(BF16)

    small[4].wait()
    small[5].wait()
    nk = nk_ref[...].astype(F32)
    nv = nv_ref[...].astype(F32)
    fresh_key = jnp.zeros((ROWS, HD), F32)
    fresh_value = jnp.zeros((ROWS, HD), F32)
    for kv in range(KVH):
        fresh_key = jnp.where(u == kv, nk[:, kv, :], fresh_key)
        fresh_value = jnp.where(u == kv, nv[:, kv, :], fresh_value)
    fresh_key = jnp.concatenate([fresh_key, fresh_key], axis=0)
    fresh_value = jnp.concatenate([fresh_value, fresh_value], axis=0)
    new_score = jnp.sum(qsend[0 : 2 * ROWS].astype(F32) * fresh_key, axis=1, keepdims=True) * SCALE

    pltpu.make_async_copy(qb, qb, recv_sem.at[0]).wait()
    ls[...] = jnp.concatenate([qb[k][2 * ROWS :].astype(F32)[0:4] for k in range(NZ)], axis=0).astype(BF16)

    chosen = jnp.dot(picks, qb[...].reshape(NZ * 48, HD), preferred_element_type=F32).astype(BF16)
    qs[...] = chosen.reshape(NP, 16, HD)

    def a2(d, carry):
        pd = lax.rem(p0 + d, NP)
        for step in range(NU):
            ud = lax.rem(u + step, NU)
            send(qs.at[pd], qr.at[p0, u], place(z0, pd, ud, w), 3, chunk_sem.at[p0])
        send(ls, lr.at[p0], place(z0, pd, u, w), 2, chunk_len_sem.at[p0])
        return carry

    lax.fori_loop(0, NP, a2, 0)
    key_copy.wait()
    value_copy.wait()

    row32 = iota((32, 2 * SUB), 0)
    lane2 = iota((32, 2 * SUB), 1)
    second = lax.rem(row32, 4) // 2
    token = jnp.where(second == lane2 // SUB, lax.rem(lane2, SUB), 1 << 20)
    second_col = lax.rem(iota((16, 1), 0), 4) // 2
    row4 = lax.rem(iota((16, HD), 0), 4)
    rest_spot = iota((16, HD), 1) - p0 * 16 - row4
    first_spot = iota((16, HD), 1) - lax.rem(u, 2) * 64 - p0 * 8 - row4
    no_query = jnp.zeros((16, HD), BF16)

    def attend(units):
        def limit(unit):
            _, coded, slot = unit
            live = []
            for s in range(PER):
                row = row_ref[0, slot + s]
                parts = jnp.where(lane1 == row, coded * 128.0, 0.0)
                parts = jnp.where(lane1 == row + ROWS, coded, parts)
                length = jnp.sum(parts, axis=1, keepdims=True).astype(jnp.int32)
                live.append(length - (blk_ref[0, slot + s] * BLK + u * SUB))
            return jnp.where(second_col == 0, live[0], live[1])

        def both(ref, pair):
            halves = [ref[pl.ds(slot, PER)].reshape(PER * SUB, HD) for _, _, slot in pair]
            return jnp.concatenate(halves, axis=1)

        results = []
        for i in range(0, len(units), 2):
            pair = units[i : i + 2]
            query = jnp.concatenate(
                [
                    jnp.concatenate([pair[0][0], no_query], axis=1),
                    jnp.concatenate([no_query, pair[1][0]], axis=1),
                ],
                axis=0,
            )
            score = (
                lax.dot_general(
                    query, both(kbuf, pair), (((1,), (1,)), ((), ())), preferred_element_type=F32
                )
                * SCALE
            )
            valid = token < jnp.concatenate([limit(pair[0]), limit(pair[1])], axis=0)
            masked = jnp.where(valid, score, LOW)
            top = jnp.max(masked, axis=1, keepdims=True)
            prob = jnp.where(valid, jnp.exp(masked - top), 0.0)
            total = jnp.sum(prob, axis=1, keepdims=True)
            out = jnp.dot(prob.astype(BF16), both(vbuf, pair), preferred_element_type=F32)
            results.append((out[:16, :HD], top[:16], total[:16]))
            results.append((out[16:, HD:], top[16:], total[16:]))
        return results

    def b1(p, results, spot, dst, recv_ref, which, recv):
        place_max = jnp.zeros((16, HD), F32)
        place_sum = jnp.zeros((16, HD), F32)
        for i, (_, top, total) in enumerate(results):
            place_max = jnp.where(spot == i * 4, top, place_max)
            place_sum = jnp.where(spot == i * 4, total, place_sum)
        for j in range(NU):
            part = slice(4 * j, 4 * j + 4)
            dst[p, j] = jnp.concatenate(
                [r[0][part] for r in results]
                + [
                    jnp.sum(place_max[part], axis=0, keepdims=True),
                    jnp.sum(place_sum[part], axis=0, keepdims=True),
                    jnp.zeros((2, HD), F32),
                ],
                axis=0,
            )

        def one(d, carry):
            j = lax.rem(u + 2 + d, NU)
            send(dst.at[p, j], recv_ref.at[u * NP + p0], place(z0, p, j, w), which, recv)
            return carry

        lax.fori_loop(0, NU, one, 0)

    def units(p, places):
        held = [qr[p, j].astype(F32) for j in range(NU)]
        coded = lr[p].astype(F32)
        found = []
        for zz in places:
            query = jnp.concatenate([x[4 * zz : 4 * zz + 4] for x in held], axis=0).astype(BF16)
            found.append((query, coded[4 * zz : 4 * zz + 1], (zz * NP + p) * PER))
        return found

    def first_chunk(d, carry):
        ps = [lax.rem(p0 + NP - 4 * d - i, NP) for i in range(4)]
        wanted = []
        for p in ps:
            pltpu.make_async_copy(qr.at[p], qr.at[p], chunk_sem.at[p]).wait()
            pltpu.make_async_copy(lr.at[p], lr.at[p], chunk_len_sem.at[p]).wait()
            wanted += units(p, FIRST)
        for p, result in zip(ps, attend(wanted)):
            b1(p, [result], first_spot, first_o, first_r, 4, recv_sem.at[2])
        return carry

    lax.fori_loop(0, NP // 4, first_chunk, 0)

    def rest_chunk(d, carry):
        ps = [lax.rem(p0 + NP - 2 * d - i, NP) for i in range(2)]
        results = attend(units(ps[0], REST) + units(ps[1], REST))
        b1(ps[0], results[: len(REST)], rest_spot, rest_o, rest_r, 5, recv_sem.at[3])
        b1(ps[1], results[len(REST) :], rest_spot, rest_o, rest_r, 5, recv_sem.at[3])
        return carry

    lax.fori_loop(0, NP // 2, rest_chunk, 0)

    sub32 = iota((32, HD), 0)
    lane32 = iota((32, HD), 1)

    def combine(places, match, blocks, stat):
        tops, sums = [], []
        for x in blocks:
            stats = jnp.sum(x, axis=0)
            tops.append(jnp.where(match, stats[stat : stat + 1], LOW))
            sums.append(stats[stat + 1 : stat + 2])
        top = tops[0]
        for x in tops[1:]:
            top = jnp.maximum(top, x)
        top = jnp.max(top, axis=1, keepdims=True)
        weights = [jnp.where(match, jnp.exp(x - top), 0.0) for x in tops]
        total = jnp.sum(sum(x * y for x, y in zip(weights, sums)), axis=1, keepdims=True)
        weights = jnp.concatenate(weights, axis=1)
        high = weights.astype(BF16)
        low = (weights - high.astype(F32)).astype(BF16)
        weights = jnp.concatenate([high, low], axis=0)
        blocks = jnp.concatenate([x.reshape(HD, HD) for x in blocks], axis=0)
        high = blocks.astype(BF16)
        low = (blocks - high.astype(F32)).astype(BF16)
        blocks = jnp.concatenate([high, low], axis=1)
        both = jnp.dot(weights, blocks, preferred_element_type=F32)
        size = 32 * len(places)
        out = both[:size, :HD] + (both[:size, HD:] + both[size:, :HD])
        for i, zz in enumerate(places):
            part = slice(32 * i, 32 * i + 32)
            fos[zz] = out[part]
            packed = jnp.where(lane32 == sub32, top[part], 0.0)
            packed = jnp.where(lane32 == 32 + sub32, total[part], packed)
            fss[zz] = jnp.sum(packed, axis=0, keepdims=True)
            target = place(zz, p0, w, u)
            send(fos.at[zz], fo.at[z0], target, 6, recv_sem.at[4])
            send(fss.at[zz], fs.at[z0], target, 7, recv_sem.at[5])

    match = jnp.logical_and(
        lax.rem(lane32, 8) < 4,
        jnp.logical_and(sub32 // 16 == lax.rem(lane32, 2), lax.rem(sub32, 16) == first_rows),
    )
    pltpu.make_async_copy(first_r, first_r, recv_sem.at[2]).wait()
    combine(FIRST, match, [first_r[b * 2 * NP : (b + 1) * 2 * NP] for b in range(NU // 2)], 4)

    sub96 = iota((96, HD), 0)
    lane96 = iota((96, HD), 1)
    match = jnp.logical_and(
        sub96 // 32 == lax.rem(lane96, 16) // 4,
        jnp.logical_and(lax.rem(sub96 // 16, 2) == lax.rem(lane96, 2), lax.rem(sub96, 16) == rest_rows),
    )
    pltpu.make_async_copy(rest_r, rest_r, recv_sem.at[3]).wait()
    combine(REST, match, [rest_r[b * NP : (b + 1) * NP] for b in range(NU)], 12)

    pltpu.make_async_copy(fs, fs, recv_sem.at[5]).wait()
    part_tops, part_sums = [], []
    for k in range(NZ):
        part_tops.append(jnp.sum(jnp.where(lane32 == sub32, fs[k], 0.0), axis=1, keepdims=True))
        part_sums.append(jnp.sum(jnp.where(lane32 == 32 + sub32, fs[k], 0.0), axis=1, keepdims=True))
    last_top = new_score
    for m in part_tops:
        last_top = jnp.maximum(last_top, m)
    fresh = jnp.exp(new_score - last_top)
    denom = fresh
    numer = fresh * fresh_value
    factors = [jnp.exp(m - last_top) for m in part_tops]
    for k in range(NZ):
        denom += factors[k] * part_sums[k]
    pltpu.make_async_copy(fo, fo, recv_sem.at[4]).wait()
    for k in range(NZ):
        numer += factors[k] * fo[k]
    result = (numer / denom).astype(BF16)
    out_ref[:, 0:HD] = result[0:ROWS]
    out_ref[:, HD : 2 * HD] = result[ROWS : 2 * ROWS]

    def sent(ref, which):
        pltpu.make_async_copy(ref, ref, send_sem.at[which]).wait()

    def sent_unless_diagonal(ref, which):
        @pl.when(jnp.logical_not(diagonal))
        def _():
            sent(ref, which)

    sent(qb.at[pl.ds(0, NZ - 1)], 0)
    sent_unless_diagonal(qsend, 0)
    sent(tb.at[pl.ds(0, NP - 1)], 1)
    sent(lr.at[pl.ds(0, NP - 1)], 2)
    sent(qr.at[pl.ds(0, NP - 1)], 3)
    sent(qr.at[0, pl.ds(0, NU - 1)], 3)
    sent(first_r.at[pl.ds(0, NP * NU - 1)], 4)
    sent(rest_r.at[pl.ds(0, NP * NU - 1)], 5)
    sent(fo.at[pl.ds(0, NZ - 1)], 6)
    sent_unless_diagonal(fo.at[0], 6)
    sent(fs.at[pl.ds(0, NZ - 1)], 7)
    sent_unless_diagonal(fs.at[0], 7)


def on_device(queries, new_key, new_value, lengths, slot_row, slot_block, key_cache, value_cache):
    hbm = pl.BlockSpec(memory_space=pltpu.HBM)
    slots = NZ * NP * PER
    return pl.pallas_call(
        kernel,
        out_shape=jax.ShapeDtypeStruct((ROWS, 2 * HD), BF16),
        in_specs=[hbm] * 8,
        out_specs=pl.BlockSpec(memory_space=pltpu.VMEM),
        scratch_shapes=[
            pltpu.VMEM((ROWS, 2 * HD), BF16),
            pltpu.VMEM((ROWS, KVH, HD), BF16),
            pltpu.VMEM((ROWS, KVH, HD), BF16),
            pltpu.SMEM((ROWS,), jnp.int32),
            pltpu.SMEM((1, slots), jnp.int32),
            pltpu.SMEM((1, slots), jnp.int32),
            pltpu.VMEM((slots, SUB, HD), BF16),
            pltpu.VMEM((slots, SUB, HD), BF16),
            pltpu.VMEM((3 * ROWS, HD), BF16),
            pltpu.VMEM((NZ, 3 * ROWS, HD), BF16),
            pltpu.VMEM((NP, 2, HD), jnp.int32),
            pltpu.VMEM((NP, 2, HD), jnp.int32),
            pltpu.VMEM((NP, 16, HD), BF16),
            pltpu.VMEM((16, HD), BF16),
            pltpu.VMEM((NP, NU, 16, HD), BF16),
            pltpu.VMEM((NP, 16, HD), BF16),
            pltpu.VMEM((NP, NU, 8, HD), F32),
            pltpu.VMEM((NP, NU, 16, HD), F32),
            pltpu.VMEM((NU * NP, 8, HD), F32),
            pltpu.VMEM((NU * NP, 16, HD), F32),
            pltpu.VMEM((NZ, 32, HD), F32),
            pltpu.VMEM((NZ, 1, HD), F32),
            pltpu.VMEM((NZ, 32, HD), F32),
            pltpu.VMEM((NZ, 1, HD), F32),
            pltpu.SemaphoreType.DMA((8,)),
            pltpu.SemaphoreType.DMA((8,)),
            pltpu.SemaphoreType.DMA((6,)),
            pltpu.SemaphoreType.DMA((NP,)),
            pltpu.SemaphoreType.DMA((NP,)),
        ],
        compiler_params=pltpu.CompilerParams(
            collective_id=0, has_side_effects=True, vmem_limit_bytes=60 * 1024 * 1024
        ),
        cost_estimate=pl.CostEstimate(flops=2 * 2 * 2 * 8 * slots * SUB * HD, bytes_accessed=2 * slots * SUB * HD * 2, transcendentals=slots * 16 * SUB),
    )(queries, new_key, new_value, lengths, slot_row, slot_block, key_cache, value_cache)


def solution(mesh):
    in_specs = (
        P("group", "tp"),
        P("group", None, None),
        P("group", None, None),
        P("group"),
        P("group", None),
        P("group", None),
        P("group", None, "tp", None, None),
        P("group", None, "tp", None, None),
    )
    return jax.shard_map(
        on_device, mesh=mesh, in_specs=in_specs, out_specs=P("group", "tp"), check_vma=False
    )
```

```python
import functools

import jax
import jax.numpy as jnp
from jax import lax
from jax.experimental import pallas as pl
from jax.experimental.pallas import tpu as pltpu
from jax.sharding import PartitionSpec as P

QH = 32
KVH = 4
HD = 128
BLK = 512
SUB = 128
NZ = 4
NP = 8
NU = 4
NW = 4
ROWS = 16
PER = 2
FIRST = (0,)
REST = (1, 2, 3)
SCALE = HD ** (-0.5)
LOW = -1e30
MESH = pl.DeviceIdType.MESH
F32 = jnp.float32
BF16 = jnp.bfloat16


def iota(shape, dim):
    return lax.broadcasted_iota(jnp.int32, shape, dim)


def kernel(
    q_hbm, nk_hbm, nv_hbm, len_hbm, row_hbm, blk_hbm, key_hbm, value_hbm, out_ref,
    q_ref, nk_ref, nv_ref, len_ref, row_ref, blk_ref, kbuf, vbuf,
    qsend, qb, lsend, lb, tsend, tb, qs, qr, lr, first_o, rest_o, first_r, rest_r, fos, fss, fo, fs,
    local_sem, send_sem, recv_sem, chunk_sem, chunk_len_sem,
):
    g = lax.axis_index("group")
    t = lax.axis_index("tp")
    z0, p0 = g // NP, lax.rem(g, NP)
    u, w = t // NW, lax.rem(t, NW)
    diagonal = u == w

    def place(zz, pp, uu, ww):
        return (zz * NP + pp, uu * NW + ww)

    barrier = pltpu.get_barrier_semaphore()

    def greet(target):
        pl.semaphore_signal(barrier, inc=1, device_id=target, device_id_type=MESH)

    for step in (2, 1, 3):
        greet(place(lax.rem(z0 + step, NZ), p0, w, u))

    @pl.when(jnp.logical_not(diagonal))
    def _():
        greet(place(z0, p0, w, u))

    small = [
        pltpu.make_async_copy(src, dst, local_sem.at[i])
        for i, (src, dst) in enumerate(
            ((q_hbm, q_ref), (len_hbm, len_ref), (row_hbm, row_ref), (blk_hbm, blk_ref), (nk_hbm, nk_ref), (nv_hbm, nv_ref))
        )
    ]
    key_copy = pltpu.make_async_copy(key_hbm.at[0, :, 0], kbuf, local_sem.at[6])
    value_copy = pltpu.make_async_copy(value_hbm.at[0, :, 0], vbuf, local_sem.at[7])
    for copy in small[:4]:
        copy.start()

    def greet_plane(d, carry):
        greet(place(z0, lax.rem(p0 + d, NP), u, w))
        return carry

    lax.fori_loop(1, NP, greet_plane, 0)
    for d in range(1, NU):
        greet(place(z0, p0, lax.rem(u + d, NU), w))
    for copy in (*small[4:], key_copy, value_copy):
        copy.start()
    for copy in small[:4]:
        copy.wait()

    first_r[:, 6:8] = jnp.zeros((NU * NP, 2, HD), F32)
    rest_r[:, 14:16] = jnp.zeros((NU * NP, 2, HD), F32)
    qsend[0:ROWS, :] = q_ref[:, 0:HD]
    qsend[ROWS : 2 * ROWS, :] = q_ref[:, HD : 2 * HD]
    lane1 = iota((1, HD), 1)
    lens = jnp.zeros((1, HD), jnp.int32)
    for r in range(ROWS):
        lens = jnp.where(lane1 == r, len_ref[r], lens)
    lsend[...] = lens
    first_spot = jnp.where(lax.rem(lane1, 8) < 4, lax.rem(lane1, 64) // 2, -1)
    for p in range(NP):
        first_row = jnp.zeros((1, HD), jnp.int32)
        rest_row = jnp.zeros((1, HD), jnp.int32)
        for s in range(PER):
            first_row = jnp.where(first_spot == p0 * 4 + s, row_ref[0, p * PER + s], first_row)
            for i, zz in enumerate(REST):
                rest_row = jnp.where(
                    lane1 // 2 == p0 * 8 + i * 2 + s, row_ref[0, (zz * NP + p) * PER + s], rest_row
                )
        tsend[p] = jnp.concatenate([first_row, rest_row], axis=0)

    pl.semaphore_wait(barrier, NZ + NP - 1 + NU - 1 - jnp.where(diagonal, 1, 0))

    def send_away(src, dst, target, which, recv):
        pltpu.make_async_remote_copy(
            src_ref=src,
            dst_ref=dst,
            send_sem=send_sem.at[which],
            recv_sem=recv,
            device_id=target,
            device_id_type=MESH,
        ).start()

    def send(src, dst, target, which, recv, here):
        @pl.when(jnp.logical_not(here))
        def _():
            send_away(src, dst, target, which, recv)

        @pl.when(here)
        def _():
            pltpu.make_async_copy(src, dst, recv).start()

    for step in (2, 1, 3, 0):
        target = place(lax.rem(z0 + step, NZ), p0, w, u)
        if step:
            send_away(qsend, qb.at[z0], target, 0, recv_sem.at[0])
            send_away(lsend, lb.at[z0], target, 8, recv_sem.at[6])
        else:
            send(qsend, qb.at[z0], target, 0, recv_sem.at[0], diagonal)
            send(lsend, lb.at[z0], target, 8, recv_sem.at[6], diagonal)

    def table(d, carry):
        pd = lax.rem(p0 + d, NP)
        send_away(tsend.at[pd], tb.at[p0], place(z0, pd, u, w), 1, recv_sem.at[1])
        return carry

    lax.fori_loop(1, NP, table, 0)
    pltpu.make_async_copy(tsend.at[p0], tb.at[p0], recv_sem.at[1]).start()
    pltpu.make_async_copy(tb, tb, recv_sem.at[1]).wait()

    rows = jnp.sum(tb[...], axis=0)
    first_rows, rest_rows = rows[0:1], rows[1:2]
    sub = iota((HD, HD), 0)
    lane = iota((HD, HD), 1)
    at = (sub // 16) * 8 + lax.rem(sub, 16)
    first_wanted = jnp.sum(jnp.where(lane == at, first_rows, 0), axis=1, keepdims=True)
    rest_wanted = jnp.sum(jnp.where(lane == sub - 4, rest_rows, 0), axis=1, keepdims=True)
    wanted = jnp.where(lax.rem(iota((HD, 1), 0), 16) < 4, first_wanted, rest_wanted)
    at = (lax.rem(sub, 16) // 4) * 32 + lax.rem(sub, 2) * ROWS + wanted
    picks = jnp.where(lane == at, 1.0, 0.0).astype(BF16)

    small[4].wait()
    small[5].wait()
    nk = nk_ref[...].astype(F32)
    nv = nv_ref[...].astype(F32)
    fresh_key = jnp.zeros((ROWS, HD), F32)
    fresh_value = jnp.zeros((ROWS, HD), F32)
    for kv in range(KVH):
        fresh_key = jnp.where(u == kv, nk[:, kv, :], fresh_key)
        fresh_value = jnp.where(u == kv, nv[:, kv, :], fresh_value)
    fresh_key = jnp.concatenate([fresh_key, fresh_key], axis=0)
    fresh_value = jnp.concatenate([fresh_value, fresh_value], axis=0)
    new_score = jnp.sum(qsend[...].astype(F32) * fresh_key, axis=1, keepdims=True) * SCALE

    pltpu.make_async_copy(qb, qb, recv_sem.at[0]).wait()
    chosen = jnp.dot(picks, qb[...].reshape(HD, HD), preferred_element_type=F32).astype(BF16)
    qs[...] = chosen.reshape(NP, 16, HD)
    pltpu.make_async_copy(lb, lb, recv_sem.at[6]).wait()

    def a2(d, carry):
        pd = lax.rem(p0 + d, NP)
        for step in range(NU):
            ud = lax.rem(u + step, NU)
            send_away(qs.at[pd], qr.at[p0, u], place(z0, pd, ud, w), 3, chunk_sem.at[p0])
        send_away(lb, lr.at[p0], place(z0, pd, u, w), 2, chunk_len_sem.at[p0])
        return carry

    for step in range(1, NU):
        send_away(qs.at[p0], qr.at[p0, u], place(z0, p0, lax.rem(u + step, NU), w), 3, chunk_sem.at[p0])
    lax.fori_loop(1, NP, a2, 0)
    pltpu.make_async_copy(qs.at[p0], qr.at[p0, u], chunk_sem.at[p0]).start()
    pltpu.make_async_copy(lb, lr.at[p0], chunk_len_sem.at[p0]).start()
    key_copy.wait()
    value_copy.wait()

    row32 = iota((32, 2 * SUB), 0)
    lane2 = iota((32, 2 * SUB), 1)
    second = lax.rem(row32, 4) // 2
    token = jnp.where(second == lane2 // SUB, lax.rem(lane2, SUB), 1 << 20)
    second_col = lax.rem(iota((16, 1), 0), 4) // 2
    row4 = lax.rem(iota((16, HD), 0), 4)
    rest_spot = iota((16, HD), 1) - p0 * 16 - row4
    first_spot = iota((16, HD), 1) - lax.rem(u, 2) * 64 - p0 * 8 - row4
    no_query = jnp.zeros((16, HD), BF16)

    def attend(units):
        def limit(unit):
            _, lengths, slot = unit
            live = []
            for s in range(PER):
                row = row_ref[0, slot + s]
                length = jnp.sum(jnp.where(lane1 == row, lengths, 0), axis=1, keepdims=True)
                live.append(length - (blk_ref[0, slot + s] * BLK + u * SUB))
            return jnp.where(second_col == 0, live[0], live[1])

        def both(ref, pair):
            halves = [ref[pl.ds(slot, PER)].reshape(PER * SUB, HD) for _, _, slot in pair]
            return jnp.concatenate(halves, axis=1)

        results = []
        for i in range(0, len(units), 2):
            pair = units[i : i + 2]
            query = jnp.concatenate(
                [
                    jnp.concatenate([pair[0][0], no_query], axis=1),
                    jnp.concatenate([no_query, pair[1][0]], axis=1),
                ],
                axis=0,
            )
            score = (
                lax.dot_general(
                    query, both(kbuf, pair), (((1,), (1,)), ((), ())), preferred_element_type=F32
                )
                * SCALE
            )
            valid = token < jnp.concatenate([limit(pair[0]), limit(pair[1])], axis=0)
            masked = jnp.where(valid, score, LOW)
            top = jnp.max(masked, axis=1, keepdims=True)
            prob = jnp.where(valid, jnp.exp(masked - top), 0.0)
            total = jnp.sum(prob, axis=1, keepdims=True)
            out = jnp.dot(prob.astype(BF16), both(vbuf, pair), preferred_element_type=F32)
            results.append((out[:16, :HD], top[:16], total[:16]))
            results.append((out[16:, HD:], top[16:], total[16:]))
        return results

    def b1(p, results, spot, dst, recv_ref, which, recv):
        used = pl.ds(0, 4 * len(results) + 2)
        place_max = jnp.zeros((16, HD), F32)
        place_sum = jnp.zeros((16, HD), F32)
        for i, (_, top, total) in enumerate(results):
            place_max = jnp.where(spot == i * 4, top, place_max)
            place_sum = jnp.where(spot == i * 4, total, place_sum)
        for j in range(NU):
            part = slice(4 * j, 4 * j + 4)
            dst[p, j] = jnp.concatenate(
                [r[0][part] for r in results]
                + [
                    jnp.sum(place_max[part], axis=0, keepdims=True),
                    jnp.sum(place_sum[part], axis=0, keepdims=True),
                    jnp.zeros((2, HD), F32),
                ],
                axis=0,
            )

        for step in (2, 1, 3):
            j = lax.rem(u + step, NU)
            send_away(dst.at[p, j, used], recv_ref.at[u * NP + p0, used], place(z0, p, j, w), which, recv)
        send(dst.at[p, u, used], recv_ref.at[u * NP + p0, used], place(z0, p, u, w), which, recv, p == p0)

    def units(p, places):
        held = [qr[p, j].astype(F32) for j in range(NU)]
        found = []
        for zz in places:
            query = jnp.concatenate([x[4 * zz : 4 * zz + 4] for x in held], axis=0).astype(BF16)
            found.append((query, lr[p, zz], (zz * NP + p) * PER))
        return found

    def first_chunk(d, carry):
        ps = [lax.rem(p0 + NP - 4 * d - i, NP) for i in range(4)]
        wanted = []
        for p in ps:
            pltpu.make_async_copy(qr.at[p], qr.at[p], chunk_sem.at[p]).wait()
            pltpu.make_async_copy(lr.at[p], lr.at[p], chunk_len_sem.at[p]).wait()
            wanted += units(p, FIRST)
        for p, result in zip(ps, attend(wanted)):
            b1(p, [result], first_spot, first_o, first_r, 4, recv_sem.at[2])
        return carry

    lax.fori_loop(0, NP // 4, first_chunk, 0)

    def rest_chunk(d, carry):
        ps = [lax.rem(p0 + NP - 2 * d - i, NP) for i in range(2)]
        results = attend(units(ps[0], REST) + units(ps[1], REST))
        b1(ps[0], results[: len(REST)], rest_spot, rest_o, rest_r, 5, recv_sem.at[3])
        b1(ps[1], results[len(REST) :], rest_spot, rest_o, rest_r, 5, recv_sem.at[3])
        return carry

    lax.fori_loop(0, NP // 2, rest_chunk, 0)

    sub32 = iota((32, HD), 0)
    lane32 = iota((32, HD), 1)

    def combine(places, match, blocks, stat):
        tops, sums = [], []
        for x in blocks:
            stats = jnp.sum(x, axis=0)
            tops.append(jnp.where(match, stats[stat : stat + 1], LOW))
            sums.append(stats[stat + 1 : stat + 2])
        top = tops[0]
        for x in tops[1:]:
            top = jnp.maximum(top, x)
        top = jnp.max(top, axis=1, keepdims=True)
        weights = [jnp.where(match, jnp.exp(x - top), 0.0) for x in tops]
        total = jnp.sum(sum(x * y for x, y in zip(weights, sums)), axis=1, keepdims=True)
        weights = jnp.concatenate(weights, axis=1)
        high = weights.astype(BF16)
        low = (weights - high.astype(F32)).astype(BF16)
        weights = jnp.concatenate([high, low], axis=0)
        blocks = jnp.concatenate([x.reshape(HD, HD) for x in blocks], axis=0)
        high = blocks.astype(BF16)
        low = (blocks - high.astype(F32)).astype(BF16)
        blocks = jnp.concatenate([high, low], axis=1)
        both = jnp.dot(weights, blocks, preferred_element_type=F32)
        size = 32 * len(places)
        out = both[:size, :HD] + (both[:size, HD:] + both[size:, :HD])
        for i, zz in enumerate(places):
            part = slice(32 * i, 32 * i + 32)
            fos[zz] = out[part]
            packed = jnp.where(lane32 == sub32, top[part], 0.0)
            packed = jnp.where(lane32 == 32 + sub32, total[part], packed)
            fss[zz] = jnp.sum(packed, axis=0, keepdims=True)
            target = place(zz, p0, w, u)
            here = jnp.logical_and(diagonal, z0 == zz)
            send(fss.at[zz], fs.at[z0], target, 7, recv_sem.at[5], here)
            send(fos.at[zz], fo.at[z0], target, 6, recv_sem.at[4], here)

    match = jnp.logical_and(
        lax.rem(lane32, 8) < 4,
        jnp.logical_and(sub32 // 16 == lax.rem(lane32, 2), lax.rem(sub32, 16) == first_rows),
    )
    arrived = first_r.at[:, pl.ds(0, 6)]
    pltpu.make_async_copy(arrived, arrived, recv_sem.at[2]).wait()
    combine(FIRST, match, [first_r[b * 2 * NP : (b + 1) * 2 * NP] for b in range(NU // 2)], 4)

    sub96 = iota((96, HD), 0)
    lane96 = iota((96, HD), 1)
    match = jnp.logical_and(
        sub96 // 32 == lax.rem(lane96, 16) // 4,
        jnp.logical_and(lax.rem(sub96 // 16, 2) == lax.rem(lane96, 2), lax.rem(sub96, 16) == rest_rows),
    )
    arrived = rest_r.at[:, pl.ds(0, 14)]
    pltpu.make_async_copy(arrived, arrived, recv_sem.at[3]).wait()
    combine(REST, match, [rest_r[b * NP : (b + 1) * NP] for b in range(NU)], 12)

    pltpu.make_async_copy(fs, fs, recv_sem.at[5]).wait()
    part_tops, part_sums = [], []
    for k in range(NZ):
        part_tops.append(jnp.sum(jnp.where(lane32 == sub32, fs[k], 0.0), axis=1, keepdims=True))
        part_sums.append(jnp.sum(jnp.where(lane32 == 32 + sub32, fs[k], 0.0), axis=1, keepdims=True))
    last_top = new_score
    for m in part_tops:
        last_top = jnp.maximum(last_top, m)
    fresh = jnp.exp(new_score - last_top)
    denom = fresh
    numer = fresh * fresh_value
    factors = [jnp.exp(m - last_top) for m in part_tops]
    for k in range(NZ):
        denom += factors[k] * part_sums[k]
    pltpu.make_async_copy(fo, fo, recv_sem.at[4]).wait()
    for k in range(NZ):
        numer += factors[k] * fo[k]
    result = (numer / denom).astype(BF16)
    out_ref[:, 0:HD] = result[0:ROWS]
    out_ref[:, HD : 2 * HD] = result[ROWS : 2 * ROWS]

    def sent(ref, which):
        pltpu.make_async_copy(ref, ref, send_sem.at[which]).wait()

    def sent_unless_diagonal(ref, which):
        @pl.when(jnp.logical_not(diagonal))
        def _():
            sent(ref, which)

    sent(qb.at[pl.ds(0, NZ - 1)], 0)
    sent_unless_diagonal(qsend, 0)
    sent(lb.at[pl.ds(0, NZ - 1)], 8)
    sent_unless_diagonal(lsend, 8)
    sent(tb.at[pl.ds(0, NP - 1)], 1)
    sent(lr.at[pl.ds(0, NP - 1)], 2)
    sent(qr.at[pl.ds(0, NP - 1)], 3)
    sent(qr.at[0, pl.ds(0, NU - 1)], 3)
    sent(first_r.at[pl.ds(0, NP * NU - 1), pl.ds(0, 6)], 4)
    sent(rest_r.at[pl.ds(0, NP * NU - 1), pl.ds(0, 14)], 5)
    sent(fo.at[pl.ds(0, NZ - 1)], 6)
    sent_unless_diagonal(fo.at[0], 6)
    sent(fs.at[pl.ds(0, NZ - 1)], 7)
    sent_unless_diagonal(fs.at[0], 7)


def on_device(queries, new_key, new_value, lengths, slot_row, slot_block, key_cache, value_cache):
    hbm = pl.BlockSpec(memory_space=pltpu.HBM)
    slots = NZ * NP * PER
    return pl.pallas_call(
        kernel,
        out_shape=jax.ShapeDtypeStruct((ROWS, 2 * HD), BF16),
        in_specs=[hbm] * 8,
        out_specs=pl.BlockSpec(memory_space=pltpu.VMEM),
        scratch_shapes=[
            pltpu.VMEM((ROWS, 2 * HD), BF16),
            pltpu.VMEM((ROWS, KVH, HD), BF16),
            pltpu.VMEM((ROWS, KVH, HD), BF16),
            pltpu.SMEM((ROWS,), jnp.int32),
            pltpu.SMEM((1, slots), jnp.int32),
            pltpu.SMEM((1, slots), jnp.int32),
            pltpu.VMEM((slots, SUB, HD), BF16),
            pltpu.VMEM((slots, SUB, HD), BF16),
            pltpu.VMEM((2 * ROWS, HD), BF16),
            pltpu.VMEM((NZ, 2 * ROWS, HD), BF16),
            pltpu.VMEM((1, HD), jnp.int32),
            pltpu.VMEM((NZ, 1, HD), jnp.int32),
            pltpu.VMEM((NP, 2, HD), jnp.int32),
            pltpu.VMEM((NP, 2, HD), jnp.int32),
            pltpu.VMEM((NP, 16, HD), BF16),
            pltpu.VMEM((NP, NU, 16, HD), BF16),
            pltpu.VMEM((NP, NZ, 1, HD), jnp.int32),
            pltpu.VMEM((NP, NU, 8, HD), F32),
            pltpu.VMEM((NP, NU, 16, HD), F32),
            pltpu.VMEM((NU * NP, 8, HD), F32),
            pltpu.VMEM((NU * NP, 16, HD), F32),
            pltpu.VMEM((NZ, 32, HD), F32),
            pltpu.VMEM((NZ, 1, HD), F32),
            pltpu.VMEM((NZ, 32, HD), F32),
            pltpu.VMEM((NZ, 1, HD), F32),
            pltpu.SemaphoreType.DMA((8,)),
            pltpu.SemaphoreType.DMA((9,)),
            pltpu.SemaphoreType.DMA((7,)),
            pltpu.SemaphoreType.DMA((NP,)),
            pltpu.SemaphoreType.DMA((NP,)),
        ],
        compiler_params=pltpu.CompilerParams(
            collective_id=0, has_side_effects=True, vmem_limit_bytes=60 * 1024 * 1024
        ),
        cost_estimate=pl.CostEstimate(flops=2 * 2 * 2 * 8 * slots * SUB * HD, bytes_accessed=2 * slots * SUB * HD * 2, transcendentals=slots * 16 * SUB),
    )(queries, new_key, new_value, lengths, slot_row, slot_block, key_cache, value_cache)


def solution(mesh):
    in_specs = (
        P("group", "tp"),
        P("group", None, None),
        P("group", None, None),
        P("group"),
        P("group", None),
        P("group", None),
        P("group", None, "tp", None, None),
        P("group", None, "tp", None, None),
    )
    return jax.shard_map(
        on_device, mesh=mesh, in_specs=in_specs, out_specs=P("group", "tp"), check_vma=False
    )
```

```python
import functools

import jax
import jax.numpy as jnp
from jax import lax
from jax.experimental import pallas as pl
from jax.experimental.pallas import tpu as pltpu
from jax.sharding import PartitionSpec as P

QH = 32
KVH = 4
HD = 128
BLK = 512
SUB = 128
NZ = 4
NP = 8
NU = 4
NW = 4
ROWS = 16
PER = 2
FIRST = (0,)
REST = (1, 2, 3)
SCALE = HD ** (-0.5)
LOW = -1e30
MESH = pl.DeviceIdType.MESH
F32 = jnp.float32
BF16 = jnp.bfloat16


def iota(shape, dim):
    return lax.broadcasted_iota(jnp.int32, shape, dim)


def kernel(
    q_hbm, nk_hbm, nv_hbm, len_hbm, row_hbm, blk_hbm, key_hbm, value_hbm, out_ref,
    q_ref, nk_ref, nv_ref, len_ref, row_ref, blk_ref, kbuf, vbuf,
    qsend, qb, lsend, lb, tsend, tb, qs, qr, lr, first_o, rest_o, first_r, rest_r, fos, fss, fo, fs,
    local_sem, send_sem, recv_sem, chunk_sem, chunk_len_sem,
):
    g = lax.axis_index("group")
    t = lax.axis_index("tp")
    z0, p0 = g // NP, lax.rem(g, NP)
    u, w = t // NW, lax.rem(t, NW)
    diagonal = u == w

    def place(zz, pp, uu, ww):
        return (zz * NP + pp, uu * NW + ww)

    barrier = pltpu.get_barrier_semaphore()

    def greet(target):
        pl.semaphore_signal(barrier, inc=1, device_id=target, device_id_type=MESH)

    for step in (2, 1, 3):
        greet(place(lax.rem(z0 + step, NZ), p0, w, u))

    @pl.when(jnp.logical_not(diagonal))
    def _():
        greet(place(z0, p0, w, u))

    small = [
        pltpu.make_async_copy(src, dst, local_sem.at[i])
        for i, (src, dst) in enumerate(
            ((q_hbm, q_ref), (len_hbm, len_ref), (row_hbm, row_ref), (blk_hbm, blk_ref), (nk_hbm, nk_ref), (nv_hbm, nv_ref))
        )
    ]
    key_copy = pltpu.make_async_copy(key_hbm.at[0, :, 0], kbuf, local_sem.at[6])
    value_copy = pltpu.make_async_copy(value_hbm.at[0, :, 0], vbuf, local_sem.at[7])
    for copy in small[:4]:
        copy.start()

    def greet_plane(d, carry):
        greet(place(z0, lax.rem(p0 + d, NP), u, w))
        return carry

    lax.fori_loop(1, NP, greet_plane, 0)
    for d in range(1, NU):
        greet(place(z0, p0, lax.rem(u + d, NU), w))
    for copy in (*small[4:], key_copy, value_copy):
        copy.start()
    for copy in small[:4]:
        copy.wait()

    first_r[:, 6:8] = jnp.zeros((NU * NP, 2, HD), F32)
    rest_r[:, 14:16] = jnp.zeros((NU * NP, 2, HD), F32)
    qsend[0:ROWS, :] = q_ref[:, 0:HD]
    qsend[ROWS : 2 * ROWS, :] = q_ref[:, HD : 2 * HD]
    lane1 = iota((1, HD), 1)
    lens = jnp.zeros((1, HD), jnp.int32)
    for r in range(ROWS):
        lens = jnp.where(lane1 == r, len_ref[r], lens)
    lsend[...] = lens
    first_spot = jnp.where(lax.rem(lane1, 8) < 4, lax.rem(lane1, 64) // 2, -1)
    for p in range(NP):
        first_row = jnp.zeros((1, HD), jnp.int32)
        rest_row = jnp.zeros((1, HD), jnp.int32)
        for s in range(PER):
            first_row = jnp.where(first_spot == p0 * 4 + s, row_ref[0, p * PER + s], first_row)
            for i, zz in enumerate(REST):
                rest_row = jnp.where(
                    lane1 // 2 == p0 * 8 + i * 2 + s, row_ref[0, (zz * NP + p) * PER + s], rest_row
                )
        tsend[p] = jnp.concatenate([first_row, rest_row], axis=0)

    pl.semaphore_wait(barrier, NZ + NP - 1 + NU - 1 - jnp.where(diagonal, 1, 0))

    def send_away(src, dst, target, which, recv):
        pltpu.make_async_remote_copy(
            src_ref=src,
            dst_ref=dst,
            send_sem=send_sem.at[which],
            recv_sem=recv,
            device_id=target,
            device_id_type=MESH,
        ).start()

    def send(src, dst, target, which, recv, here):
        @pl.when(jnp.logical_not(here))
        def _():
            send_away(src, dst, target, which, recv)

        @pl.when(here)
        def _():
            pltpu.make_async_copy(src, dst, recv).start()

    for step in (2, 1, 3, 0):
        target = place(lax.rem(z0 + step, NZ), p0, w, u)
        if step:
            send_away(qsend, qb.at[z0], target, 0, recv_sem.at[0])
        else:
            send(qsend, qb.at[z0], target, 0, recv_sem.at[0], diagonal)
    for step in (2, 1, 3):
        send_away(lsend, lb.at[z0], place(lax.rem(z0 + step, NZ), p0, w, u), 8, recv_sem.at[6])
    send(lsend, lb.at[z0], place(z0, p0, w, u), 8, recv_sem.at[6], diagonal)

    def table(d, carry):
        pd = lax.rem(p0 + d, NP)
        send_away(tsend.at[pd], tb.at[p0], place(z0, pd, u, w), 1, recv_sem.at[1])
        return carry

    lax.fori_loop(1, NP, table, 0)
    pltpu.make_async_copy(tsend.at[p0], tb.at[p0], recv_sem.at[1]).start()
    pltpu.make_async_copy(tb, tb, recv_sem.at[1]).wait()

    rows = jnp.sum(tb[...], axis=0)
    first_rows, rest_rows = rows[0:1], rows[1:2]
    sub = iota((HD, HD), 0)
    lane = iota((HD, HD), 1)
    at = (sub // 16) * 8 + lax.rem(sub, 16)
    first_wanted = jnp.sum(jnp.where(lane == at, first_rows, 0), axis=1, keepdims=True)
    rest_wanted = jnp.sum(jnp.where(lane == sub - 4, rest_rows, 0), axis=1, keepdims=True)
    wanted = jnp.where(lax.rem(iota((HD, 1), 0), 16) < 4, first_wanted, rest_wanted)
    at = (lax.rem(sub, 16) // 4) * 32 + lax.rem(sub, 2) * ROWS + wanted
    picks = jnp.where(lane == at, 1.0, 0.0).astype(BF16)

    small[4].wait()
    small[5].wait()
    nk = nk_ref[...].astype(F32)
    nv = nv_ref[...].astype(F32)
    fresh_key = jnp.zeros((ROWS, HD), F32)
    fresh_value = jnp.zeros((ROWS, HD), F32)
    for kv in range(KVH):
        fresh_key = jnp.where(u == kv, nk[:, kv, :], fresh_key)
        fresh_value = jnp.where(u == kv, nv[:, kv, :], fresh_value)
    fresh_key = jnp.concatenate([fresh_key, fresh_key], axis=0)
    fresh_value = jnp.concatenate([fresh_value, fresh_value], axis=0)
    new_score = jnp.sum(qsend[...].astype(F32) * fresh_key, axis=1, keepdims=True) * SCALE

    pltpu.make_async_copy(qb, qb, recv_sem.at[0]).wait()
    chosen = jnp.dot(picks, qb[...].reshape(HD, HD), preferred_element_type=F32).astype(BF16)
    qs[...] = chosen.reshape(NP, 16, HD)
    pltpu.make_async_copy(lb, lb, recv_sem.at[6]).wait()

    def a2(d, carry):
        pd = lax.rem(p0 + d, NP)
        for step in (2, 1, 3, 0):
            ud = lax.rem(u + step, NU)
            send_away(qs.at[pd], qr.at[p0, u], place(z0, pd, ud, w), 3, chunk_sem.at[p0])
        send_away(lb, lr.at[p0], place(z0, pd, u, w), 2, chunk_len_sem.at[p0])
        return carry

    for step in (2, 1, 3):
        send_away(qs.at[p0], qr.at[p0, u], place(z0, p0, lax.rem(u + step, NU), w), 3, chunk_sem.at[p0])
    lax.fori_loop(1, NP, a2, 0)
    pltpu.make_async_copy(qs.at[p0], qr.at[p0, u], chunk_sem.at[p0]).start()
    pltpu.make_async_copy(lb, lr.at[p0], chunk_len_sem.at[p0]).start()
    key_copy.wait()
    value_copy.wait()

    row32 = iota((32, 2 * SUB), 0)
    lane2 = iota((32, 2 * SUB), 1)
    second = lax.rem(row32, 4) // 2
    token = jnp.where(second == lane2 // SUB, lax.rem(lane2, SUB), 1 << 20)
    second_col = lax.rem(iota((16, 1), 0), 4) // 2
    row4 = lax.rem(iota((16, HD), 0), 4)
    rest_spot = iota((16, HD), 1) - p0 * 16 - row4
    first_spot = iota((16, HD), 1) - lax.rem(u, 2) * 64 - p0 * 8 - row4
    no_query = jnp.zeros((16, HD), BF16)

    def attend(units):
        def limit(unit):
            _, lengths, slot = unit
            live = []
            for s in range(PER):
                row = row_ref[0, slot + s]
                length = jnp.sum(jnp.where(lane1 == row, lengths, 0), axis=1, keepdims=True)
                live.append(length - (blk_ref[0, slot + s] * BLK + u * SUB))
            return jnp.where(second_col == 0, live[0], live[1])

        def both(ref, pair):
            halves = [ref[pl.ds(slot, PER)].reshape(PER * SUB, HD) for _, _, slot in pair]
            return jnp.concatenate(halves, axis=1)

        results = []
        for i in range(0, len(units), 2):
            pair = units[i : i + 2]
            query = jnp.concatenate(
                [
                    jnp.concatenate([pair[0][0], no_query], axis=1),
                    jnp.concatenate([no_query, pair[1][0]], axis=1),
                ],
                axis=0,
            )
            score = (
                lax.dot_general(
                    query, both(kbuf, pair), (((1,), (1,)), ((), ())), preferred_element_type=F32
                )
                * SCALE
            )
            valid = token < jnp.concatenate([limit(pair[0]), limit(pair[1])], axis=0)
            masked = jnp.where(valid, score, LOW)
            top = jnp.max(masked, axis=1, keepdims=True)
            prob = jnp.where(valid, jnp.exp(masked - top), 0.0)
            total = jnp.sum(prob, axis=1, keepdims=True)
            out = jnp.dot(prob.astype(BF16), both(vbuf, pair), preferred_element_type=F32)
            results.append((out[:16, :HD], top[:16], total[:16]))
            results.append((out[16:, HD:], top[16:], total[16:]))
        return results

    def b1(p, results, spot, dst, recv_ref, which, recv):
        used = pl.ds(0, 4 * len(results) + 2)
        place_max = jnp.zeros((16, HD), F32)
        place_sum = jnp.zeros((16, HD), F32)
        for i, (_, top, total) in enumerate(results):
            place_max = jnp.where(spot == i * 4, top, place_max)
            place_sum = jnp.where(spot == i * 4, total, place_sum)
        for j in range(NU):
            part = slice(4 * j, 4 * j + 4)
            dst[p, j] = jnp.concatenate(
                [r[0][part] for r in results]
                + [
                    jnp.sum(place_max[part], axis=0, keepdims=True),
                    jnp.sum(place_sum[part], axis=0, keepdims=True),
                    jnp.zeros((2, HD), F32),
                ],
                axis=0,
            )

        for step in (2, 1, 3):
            j = lax.rem(u + step, NU)
            send_away(dst.at[p, j, used], recv_ref.at[u * NP + p0, used], place(z0, p, j, w), which, recv)
        send(dst.at[p, u, used], recv_ref.at[u * NP + p0, used], place(z0, p, u, w), which, recv, p == p0)

    def units(p, places):
        held = [qr[p, j].astype(F32) for j in range(NU)]
        found = []
        for zz in places:
            query = jnp.concatenate([x[4 * zz : 4 * zz + 4] for x in held], axis=0).astype(BF16)
            found.append((query, lr[p, zz], (zz * NP + p) * PER))
        return found

    def first_chunk(d, carry):
        ps = [lax.rem(p0 + NP - 2 * d - i, NP) for i in range(2)]
        wanted = []
        for p in ps:
            pltpu.make_async_copy(qr.at[p], qr.at[p], chunk_sem.at[p]).wait()
            pltpu.make_async_copy(lr.at[p], lr.at[p], chunk_len_sem.at[p]).wait()
            wanted += units(p, FIRST)
        for p, result in zip(ps, attend(wanted)):
            b1(p, [result], first_spot, first_o, first_r, 4, recv_sem.at[2])
        return carry

    lax.fori_loop(0, NP // 2, first_chunk, 0)

    def rest_chunk(d, carry):
        ps = [lax.rem(p0 + NP - 2 * d - i, NP) for i in range(2)]
        results = attend(units(ps[0], REST) + units(ps[1], REST))
        b1(ps[0], results[: len(REST)], rest_spot, rest_o, rest_r, 5, recv_sem.at[3])
        b1(ps[1], results[len(REST) :], rest_spot, rest_o, rest_r, 5, recv_sem.at[3])
        return carry

    lax.fori_loop(0, NP // 2, rest_chunk, 0)

    sub32 = iota((32, HD), 0)
    lane32 = iota((32, HD), 1)

    def prepare(blocks, stat):
        stats = [jnp.sum(x, axis=0)[stat : stat + 2] for x in blocks]
        blocks = jnp.concatenate([x.reshape(HD, HD) for x in blocks], axis=0)
        high = blocks.astype(BF16)
        low = (blocks - high.astype(F32)).astype(BF16)
        return stats, jnp.concatenate([high, low], axis=1)

    def combine(places, match, stats, blocks):
        tops = [jnp.where(match, x[0:1], LOW) for x in stats]
        top = tops[0]
        for x in tops[1:]:
            top = jnp.maximum(top, x)
        top = jnp.max(top, axis=1, keepdims=True)
        weights = [jnp.where(match, jnp.exp(x - top), 0.0) for x in tops]
        total = jnp.sum(sum(x * y[1:2] for x, y in zip(weights, stats)), axis=1, keepdims=True)
        weights = jnp.concatenate(weights, axis=1)
        high = weights.astype(BF16)
        low = (weights - high.astype(F32)).astype(BF16)
        weights = jnp.concatenate([high, low], axis=0)
        both = jnp.dot(weights, blocks, preferred_element_type=F32)
        size = 32 * len(places)
        out = both[:size, :HD] + (both[:size, HD:] + both[size:, :HD])
        for i, zz in enumerate(places):
            part = slice(32 * i, 32 * i + 32)
            fos[zz] = out[part]
            packed = jnp.where(lane32 == sub32, top[part], 0.0)
            packed = jnp.where(lane32 == 32 + sub32, total[part], packed)
            fss[zz] = jnp.sum(packed, axis=0, keepdims=True)
            target = place(zz, p0, w, u)
            here = jnp.logical_and(diagonal, z0 == zz)
            send(fss.at[zz], fs.at[z0], target, 7, recv_sem.at[5], here)
            send(fos.at[zz], fo.at[z0], target, 6, recv_sem.at[4], here)

    match = jnp.logical_and(
        lax.rem(lane32, 8) < 4,
        jnp.logical_and(sub32 // 16 == lax.rem(lane32, 2), lax.rem(sub32, 16) == first_rows),
    )
    arrived = first_r.at[:, pl.ds(0, 6)]
    pltpu.make_async_copy(arrived, arrived, recv_sem.at[2]).wait()
    combine(FIRST, match, *prepare([first_r[b * 2 * NP : (b + 1) * 2 * NP] for b in range(NU // 2)], 4))

    sub96 = iota((96, HD), 0)
    lane96 = iota((96, HD), 1)
    match = jnp.logical_and(
        sub96 // 32 == lax.rem(lane96, 16) // 4,
        jnp.logical_and(lax.rem(sub96 // 16, 2) == lax.rem(lane96, 2), lax.rem(sub96, 16) == rest_rows),
    )
    arrived = rest_r.at[:, pl.ds(0, 14)]
    pltpu.make_async_copy(arrived, arrived, recv_sem.at[3]).wait()
    prepared = prepare([rest_r[b * NP : (b + 1) * NP] for b in range(NU)], 12)
    combine(REST[:1], match[:32], *prepared)
    combine(REST[1:], match[32:], *prepared)

    pltpu.make_async_copy(fs, fs, recv_sem.at[5]).wait()
    part_tops, part_sums = [], []
    for k in range(NZ):
        part_tops.append(jnp.sum(jnp.where(lane32 == sub32, fs[k], 0.0), axis=1, keepdims=True))
        part_sums.append(jnp.sum(jnp.where(lane32 == 32 + sub32, fs[k], 0.0), axis=1, keepdims=True))
    last_top = new_score
    for m in part_tops:
        last_top = jnp.maximum(last_top, m)
    fresh = jnp.exp(new_score - last_top)
    denom = fresh
    numer = fresh * fresh_value
    factors = [jnp.exp(m - last_top) for m in part_tops]
    for k in range(NZ):
        denom += factors[k] * part_sums[k]
    pltpu.make_async_copy(fo, fo, recv_sem.at[4]).wait()
    for k in range(NZ):
        numer += factors[k] * fo[k]
    result = (numer / denom).astype(BF16)
    out_ref[:, 0:HD] = result[0:ROWS]
    out_ref[:, HD : 2 * HD] = result[ROWS : 2 * ROWS]

    def sent(ref, which):
        pltpu.make_async_copy(ref, ref, send_sem.at[which]).wait()

    def sent_unless_diagonal(ref, which):
        @pl.when(jnp.logical_not(diagonal))
        def _():
            sent(ref, which)

    sent(qb.at[pl.ds(0, NZ - 1)], 0)
    sent_unless_diagonal(qsend, 0)
    sent(lb.at[pl.ds(0, NZ - 1)], 8)
    sent_unless_diagonal(lsend, 8)
    sent(tb.at[pl.ds(0, NP - 1)], 1)
    sent(lr.at[pl.ds(0, NP - 1)], 2)
    sent(qr.at[pl.ds(0, NP - 1)], 3)
    sent(qr.at[0, pl.ds(0, NU - 1)], 3)
    sent(first_r.at[pl.ds(0, NP * NU - 1), pl.ds(0, 6)], 4)
    sent(rest_r.at[pl.ds(0, NP * NU - 1), pl.ds(0, 14)], 5)
    sent(fo.at[pl.ds(0, NZ - 1)], 6)
    sent_unless_diagonal(fo.at[0], 6)
    sent(fs.at[pl.ds(0, NZ - 1)], 7)
    sent_unless_diagonal(fs.at[0], 7)


def on_device(queries, new_key, new_value, lengths, slot_row, slot_block, key_cache, value_cache):
    hbm = pl.BlockSpec(memory_space=pltpu.HBM)
    slots = NZ * NP * PER
    return pl.pallas_call(
        kernel,
        out_shape=jax.ShapeDtypeStruct((ROWS, 2 * HD), BF16),
        in_specs=[hbm] * 8,
        out_specs=pl.BlockSpec(memory_space=pltpu.VMEM),
        scratch_shapes=[
            pltpu.VMEM((ROWS, 2 * HD), BF16),
            pltpu.VMEM((ROWS, KVH, HD), BF16),
            pltpu.VMEM((ROWS, KVH, HD), BF16),
            pltpu.SMEM((ROWS,), jnp.int32),
            pltpu.SMEM((1, slots), jnp.int32),
            pltpu.SMEM((1, slots), jnp.int32),
            pltpu.VMEM((slots, SUB, HD), BF16),
            pltpu.VMEM((slots, SUB, HD), BF16),
            pltpu.VMEM((2 * ROWS, HD), BF16),
            pltpu.VMEM((NZ, 2 * ROWS, HD), BF16),
            pltpu.VMEM((1, HD), jnp.int32),
            pltpu.VMEM((NZ, 1, HD), jnp.int32),
            pltpu.VMEM((NP, 2, HD), jnp.int32),
            pltpu.VMEM((NP, 2, HD), jnp.int32),
            pltpu.VMEM((NP, 16, HD), BF16),
            pltpu.VMEM((NP, NU, 16, HD), BF16),
            pltpu.VMEM((NP, NZ, 1, HD), jnp.int32),
            pltpu.VMEM((NP, NU, 8, HD), F32),
            pltpu.VMEM((NP, NU, 16, HD), F32),
            pltpu.VMEM((NU * NP, 8, HD), F32),
            pltpu.VMEM((NU * NP, 16, HD), F32),
            pltpu.VMEM((NZ, 32, HD), F32),
            pltpu.VMEM((NZ, 1, HD), F32),
            pltpu.VMEM((NZ, 32, HD), F32),
            pltpu.VMEM((NZ, 1, HD), F32),
            pltpu.SemaphoreType.DMA((8,)),
            pltpu.SemaphoreType.DMA((9,)),
            pltpu.SemaphoreType.DMA((7,)),
            pltpu.SemaphoreType.DMA((NP,)),
            pltpu.SemaphoreType.DMA((NP,)),
        ],
        compiler_params=pltpu.CompilerParams(
            collective_id=0, has_side_effects=True, vmem_limit_bytes=60 * 1024 * 1024
        ),
        cost_estimate=pl.CostEstimate(flops=2 * 2 * 2 * 8 * slots * SUB * HD, bytes_accessed=2 * slots * SUB * HD * 2, transcendentals=slots * 16 * SUB),
    )(queries, new_key, new_value, lengths, slot_row, slot_block, key_cache, value_cache)


def solution(mesh):
    in_specs = (
        P("group", "tp"),
        P("group", None, None),
        P("group", None, None),
        P("group"),
        P("group", None),
        P("group", None),
        P("group", None, "tp", None, None),
        P("group", None, "tp", None, None),
    )
    return jax.shard_map(
        on_device, mesh=mesh, in_specs=in_specs, out_specs=P("group", "tp"), check_vma=False
    )
```
